256 devices in a mesh: grp: 2 (over core), row: 16 (over y, z_hi), col: 8 (over x, z_lo).
Axes of the slice: x: 4, y: 4, z: 8 (z_hi: 4, z_lo: 2; z = z_hi * 2 + z_lo), core: 2. Of those that a mesh axis runs over, the one named last changes fastest.
Arguments:
- tokens: bfloat16 [1024, 16384], P('col', ('grp', 'row')), may hold values from -48 to 48
- norm_gain: bfloat16 [16384], P(('grp', 'row')), may hold values from 0.099609375 to 1.8984375
- query_weight: bfloat16 [16384, 16384], P(('grp', 'row'), 'col'), may hold values from -24 to 24
- key_weight: bfloat16 [16384, 1024], P(('grp', 'row'), 'col'), may hold values from -1 to 1
- value_weight: bfloat16 [16384, 1024], P(('grp', 'row'), 'col'), may hold values from -0.046875 to 0.046875
- output_weight: bfloat16 [16384, 16384], P('col', ('grp', 'row')), may hold values from -0.046875 to 0.046875
Outputs:
- gram: float32 [16384, 16384], P('col', ('grp', 'row'))
- cross: float32 [16384, 16384], P('col', ('grp', 'row'))
The draws below stay inside these ranges and needn't reach their ends.
All inputs are finite; a program needn't handle non-finite values.
Results may differ from the reference program's by a relative error of at most 0.015.
Values may be sent and summed in bfloat16 or wider, within the bound.
A program may use at most 128 MiB of HBM per device.

```python
import math
import jax
import jax.numpy as jnp
from jax import lax

D = 16384
H = 128
KVH = 8
HD = 128
LEN = 1024


def shared_keys(key):
    return jnp.clip(jax.random.normal(key, (D, KVH * HD), jnp.float32), -6.0, 6.0)


def draw_key_weight(key, part):
    base = shared_keys(key)
    return (base * D ** (-0.5)).astype(jnp.bfloat16)


def draw_query_weight(key, part):
    key = jax.random.fold_in(key, 1)
    noise = jnp.clip(jax.random.normal(key, (D, H * HD), jnp.float32), -6.0, 6.0) * D ** (-0.5)
    return noise.astype(jnp.bfloat16)


def draw_tokens(key, part):
    key = jax.random.fold_in(key, 3)
    core_key, row_key, col_key = jax.random.split(key, 3)
    row_scale = jnp.exp(jax.random.uniform(row_key, (LEN, 1), jnp.float32, math.log(0.3), math.log(3.0)))
    rising = 3.0 ** (jnp.arange(D, dtype=jnp.float32) / D - 0.5)
    col_scale = rising[None, :] * jnp.exp(jax.random.uniform(col_key, (1, D), jnp.float32, -0.7, 0.7))
    core = jnp.clip(jax.random.normal(core_key, (LEN, D), jnp.float32), -4.0, 4.0)
    return (core * row_scale * col_scale).astype(jnp.bfloat16)


def level_of(stream_key, shape, cuts, low, top_value):
    gain, own = 1.0, jax.random.fold_in(stream_key, 6)
    for dim, shards_of in cuts:
        draws = jnp.exp(jax.random.uniform(jax.random.fold_in(own, dim), (shards_of,), jnp.float32, low / len(cuts), top_value / len(cuts)))
        gain = gain * jnp.repeat(draws, shape[dim] // shards_of).reshape([-1 if axis == dim else 1 for axis in range(len(shape))])
    return gain


def normal_values(own_key, extent, scale, most, pieces=(), kind=jnp.bfloat16):
    values = scale * jax.random.normal(own_key, extent, jnp.float32)
    if pieces:
        values = values * level_of(own_key, extent, pieces, -0.22, 0.18)
    return jnp.clip(values, -most, most).astype(kind)


def setup_inputs(seed: int = 0) -> dict:
    arg_keys = jax.random.split(jax.random.key(seed), 7)
    tokens = draw_tokens(jax.random.fold_in(arg_keys[6], 71), 0)
    norm_gain = jnp.clip(1.0 + 0.18 * jax.random.normal(arg_keys[1], (D,), jnp.float32), 0.099609375, 1.8984375).astype(jnp.bfloat16)
    query_weight = draw_query_weight(jax.random.fold_in(arg_keys[6], 71), 0)
    key_weight = draw_key_weight(jax.random.fold_in(arg_keys[6], 71), 0)
    value_weight = normal_values(arg_keys[4], (D, KVH * HD), D ** -0.5, 0.046875, ((0, 32), (1, 8)))
    output_weight = normal_values(arg_keys[5], (H * HD, D), (H * HD) ** -0.5, 0.046875, ((0, 8), (1, 32)))
    return {"tokens": tokens, "norm_gain": norm_gain, "query_weight": query_weight, "key_weight": key_weight, "value_weight": value_weight, "output_weight": output_weight}


def rotate(values, positions):
    half = values.shape[-1] // 2
    frequency = 500000.0 ** (-jnp.arange(half, dtype=jnp.float32) * 2.0 / values.shape[-1])
    angles = positions[:, None] * frequency[None, :]
    cosine = jnp.cos(angles)[:, None, :]
    sine = jnp.sin(angles)[:, None, :]
    first = values[..., :half]
    second = values[..., half:]
    return jnp.concatenate([first * cosine - second * sine, second * cosine + first * sine], axis=-1)

def reference(tokens, norm_gain, query_weight, key_weight, value_weight, output_weight):
    wide = tokens.astype(jnp.float32)
    squares = lax.optimization_barrier(jnp.sum(wide * wide, axis=1, keepdims=True))
    normed = (wide * lax.rsqrt(squares / D + 1e-05) * norm_gain.astype(jnp.float32)).astype(jnp.bfloat16)
    queries = jnp.dot(normed, query_weight, preferred_element_type=jnp.float32).reshape(LEN, H, HD)
    keys = jnp.dot(normed, key_weight, preferred_element_type=jnp.float32).reshape(LEN, KVH, HD)
    values = jnp.dot(normed, value_weight, preferred_element_type=jnp.float32).reshape(LEN, KVH, HD)
    positions = jnp.arange(LEN, dtype=jnp.float32)
    queries = rotate(queries, positions).astype(jnp.bfloat16)
    keys = rotate(keys, positions).astype(jnp.bfloat16)
    values = values.astype(jnp.bfloat16)
    groups = H // KVH
    grouped = jnp.transpose(queries.reshape(LEN, KVH, groups, HD), (1, 2, 0, 3))
    key_heads = jnp.transpose(keys, (1, 0, 2))
    value_heads = jnp.transpose(values, (1, 0, 2))
    causal = jnp.arange(LEN)[None, :] <= jnp.arange(LEN)[:, None]

    def one_head(items):
        query_block, key_block, value_block = items
        scores = jnp.einsum('gtd,sd->gts', query_block.astype(jnp.float32), key_block.astype(jnp.float32)) / math.sqrt(HD)
        scores = jnp.where(causal[None], scores, jnp.float32(-1e+30))
        probs = jax.nn.softmax(scores, axis=-1).astype(jnp.bfloat16)
        return jnp.einsum('gts,sd->gtd', probs.astype(jnp.float32), value_block.astype(jnp.float32)).astype(jnp.bfloat16)
    attended = lax.map(one_head, (grouped, key_heads, value_heads))
    attended = jnp.transpose(attended, (2, 0, 1, 3)).reshape(LEN, H * HD)
    branch = jnp.dot(attended, output_weight, preferred_element_type=jnp.float32).astype(jnp.bfloat16)
    gram = jnp.dot(tokens.T, tokens, preferred_element_type=jnp.float32) / LEN
    cross = jnp.dot(tokens.T, branch, preferred_element_type=jnp.float32) / LEN
    return (gram, cross)
```

```python
import functools
import math

import jax
import jax.numpy as jnp
import numpy as np
from jax import lax
from jax.experimental import pallas as pl
from jax.experimental.pallas import tpu as pltpu
from jax.sharding import PartitionSpec as P

D = 16384
H = 128
HD = 128
LEN = 1024
MESH = pl.DeviceIdType.MESH
BF = jnp.bfloat16
F32 = jnp.float32
FB = 512
KVW = 384
QW = 1024
WIDTHS = (KVW, QW, QW)


def tables():
    half = HD // 2
    frequency = np.float32(500000.0) ** (-np.arange(half, dtype=np.float32) * np.float32(2.0 / HD))
    angles = np.arange(LEN, dtype=np.float32)[:, None] * frequency.astype(np.float32)[None, :]
    cosine = np.cos(angles.astype(np.float64)).astype(np.float32)
    sine = np.sin(angles.astype(np.float64)).astype(np.float32)
    return (
        np.concatenate([cosine, cosine], axis=1),
        np.concatenate([-sine, sine], axis=1),
    )


def strips(rows, step, body):
    def one(i, carry):
        body(pl.multiple_of(i * step, step))
        return carry

    lax.fori_loop(0, rows // step, one, 0)


def kernel(tok, gain, wk_in, wv_in, wq_in, wo_in, cos_in, sin_in, tf_out, panel_out, branch_out, *scratch):
    names = iter(scratch)
    nxt = lambda: next(names)
    tf, xg, sq, wkv, wq, wo, cosv, sinv = [nxt() for _ in range(8)]
    sib_send = [nxt() for _ in range(3)]
    sib_recv = [nxt() for _ in range(3)]
    r1 = [nxt() for _ in range(3)]
    y_send_p = [nxt() for _ in range(3)]
    y_send_m = [nxt() for _ in range(3)]
    y_send_f = [nxt() for _ in range(3)]
    y_recv_p = [nxt() for _ in range(3)]
    y_recv_m = [nxt() for _ in range(3)]
    y_recv_f = [nxt() for _ in range(3)]
    s2 = [nxt() for _ in range(3)]
    z_send = [nxt() for _ in range(3)]
    z_recv = [nxt() for _ in range(3)]
    kv, rs_scale, qs = [nxt() for _ in range(3)]
    att = [nxt() for _ in range(2)]
    acc, bsend, brecv, ball, panel = [nxt() for _ in range(5)]
    ssem, rsem, lsem, bssem, brsem = [nxt() for _ in range(5)]

    g = lax.axis_index("grp")
    row = lax.axis_index("row")
    c = lax.axis_index("col")
    y, zh = row // 4, row % 4
    x, zl = c // 2, c % 2

    def at_y(d):
        return {"row": ((y + d) % 4) * 4 + zh}

    def at_z(d):
        return {"row": y * 4 + (zh + d) % 4}

    def at_col(dx, dl):
        return {"col": ((x + dx) % 4) * 2 + (zl + dl) % 2}

    sibling = {"grp": 1 - g}
    col_offsets = [(0, 1), (1, 0), (3, 0), (1, 1), (3, 1), (2, 0), (2, 1)]

    local = []

    def load(src, dst):
        copy = pltpu.make_async_copy(src, dst, lsem.at[len(local)])
        copy.start()
        local.append(copy)
        return copy

    own_row = pl.multiple_of(g * 512 + y * 128 + zh * 32, 32)
    my_tokens = pl.ds(pl.multiple_of(c * 128, 128), 128)
    l_tok = load(tok, tf.at[my_tokens])
    l_k = load(wk_in, wkv.at[:, pl.ds(0, HD)])
    l_v = load(wv_in, wkv.at[:, pl.ds(HD, HD)])
    l_q = load(wq_in, wq)
    l_cos = load(cos_in.at[pl.ds(own_row, 32)], cosv)
    l_sin = load(sin_in.at[pl.ds(own_row, 32)], sinv)
    l_o = load(wo_in, wo)

    barrier = pltpu.get_barrier_semaphore()
    peers = [sibling] + [at_y(d) for d in (1, 2, 3)] + [at_z(d) for d in (1, 2, 3)]
    peers += [at_col(*o) for o in col_offsets]
    for peer in peers:
        pl.semaphore_signal(barrier, inc=1, device_id=peer, device_id_type=MESH)
    pl.semaphore_wait(barrier, len(peers))

    sends = []
    count = [0]

    def describe(src, dst, dev, index=None):
        if index is None:
            index = count[0]
            count[0] += 1
        return pltpu.make_async_remote_copy(
            src_ref=src,
            dst_ref=dst,
            send_sem=ssem.at[index],
            recv_sem=rsem.at[index],
            device_id=dev,
            device_id_type=MESH,
        )

    def send(src, dst, dev):
        copy = describe(src, dst, dev)
        copy.start()
        sends.append(copy)
        return copy

    gather = [send(tok, tf.at[my_tokens], at_col(*o)) for o in col_offsets]
    l_tok.wait()
    for copy in gather:
        copy.wait_recv()

    panel_core = g == c // 4
    delta = (y - c % 4 + 4) % 4
    is_source = jnp.logical_and(panel_core, delta == 0)
    part_a = [describe(tf, panel.at[zh], at_z(d)) for d in (1, 2, 3)]
    own_panel = pltpu.make_async_copy(tf, panel.at[zh], lsem.at[len(local)])
    local.append(None)

    @pl.when(is_source)
    def _():
        for copy in part_a:
            copy.start()
        own_panel.start()

    out_tf = pltpu.make_async_copy(tf, tf_out, lsem.at[len(local)])
    local.append(None)
    out_tf.start()

    def prepare(i):
        rows = pl.ds(i, 32)
        wide = tf[rows, :].astype(F32)
        xg[rows, :] = (wide * gain[...].astype(F32)).astype(BF)
        square = wide * wide
        sq[rows, :] = square[:, 0:128] + square[:, 128:256] + square[:, 256:384] + square[:, 384:512]

    strips(LEN, 32, prepare)

    mine = pl.multiple_of(g * 512, 512)
    theirs = pl.multiple_of((1 - g) * 512, 512)

    def project(k, base, out):
        weights, first, wide = (wkv, 0, 256) if k == 0 else (wq, (k - 1) * QW, QW)

        def tile(i):
            value = jnp.dot(
                xg[pl.ds(base, 512), :],
                weights[:, pl.ds(pl.multiple_of(first + i, 256), 256)],
                preferred_element_type=F32,
            )
            out[:, pl.ds(i, 256)] = value.astype(out.dtype)

        strips(wide, 256, tile)
        if k == 0:
            out[:, pl.ds(256, 128)] = sq[pl.ds(base, 512), :].astype(out.dtype)

    sib = [None] * 3

    def sib_stage(k):
        project(k, theirs, sib_send[k])
        sib[k] = send(sib_send[k], sib_recv[k], sibling)

    def own_stage(k):
        project(k, mine, r1[k])

    def y_rows(d):
        return pl.multiple_of(((y + d) % 4) * 128, 128)

    y_moves = [None] * 3

    def y_first(k):
        sib[k].wait_recv()

        def pair(d, dst, start, rows):
            base = y_rows(d)

            def strip(i):
                r = pl.ds(pl.multiple_of(base + start + i, 16), 16)
                dst[pl.ds(pl.multiple_of(start + i, 16), 16), :] = (r1[k][r, :] + sib_recv[k][r, :].astype(F32)).astype(BF)

            strips(rows, 16, strip)

        top, low = pl.ds(0, 64), pl.ds(64, 64)
        pair(2, y_send_f[k], 0, 128)
        m1p = send(y_send_f[k].at[top], y_recv_f[k].at[top], at_y(1))
        m1m = send(y_send_f[k].at[low], y_recv_f[k].at[low], at_y(3))
        pair(1, y_send_p[k], 64, 64)
        m2p = send(y_send_p[k].at[low], y_recv_p[k].at[low], at_y(1))
        pair(3, y_send_m[k], 0, 64)
        m2m = send(y_send_m[k].at[top], y_recv_m[k].at[top], at_y(3))
        y_moves[k] = [m1p, m1m, m2p, m2m]

    def y_second(k):
        top, low = pl.ds(0, 64), pl.ds(64, 64)
        m1p, m1m = y_moves[k][:2]

        def relay(d, dst, start):
            base = y_rows(d)

            def strip(i):
                r = pl.ds(pl.multiple_of(base + start + i, 16), 16)
                f = pl.ds(pl.multiple_of(start + i, 16), 16)
                dst[f, :] = (r1[k][r, :] + sib_recv[k][r, :].astype(F32) + y_recv_f[k][f, :].astype(F32)).astype(BF)

            strips(64, 16, strip)

        m1p.wait_recv()
        relay(1, y_send_p[k], 0)
        m3p = send(y_send_p[k].at[top], y_recv_p[k].at[top], at_y(1))
        m1m.wait_recv()
        relay(3, y_send_m[k], 64)
        m3m = send(y_send_m[k].at[low], y_recv_m[k].at[low], at_y(3))
        y_moves[k] += [m3p, m3m]

    z_moves = [None] * 3

    def z_first(k):
        for copy in y_moves[k][2:]:
            copy.wait_recv()
        base = y_rows(0)

        def strip(i):
            r = pl.ds(pl.multiple_of(base + i, 16), 16)
            f = pl.ds(i, 16)
            total = r1[k][r, :] + sib_recv[k][r, :].astype(F32) + y_recv_p[k][f, :].astype(F32) + y_recv_m[k][f, :].astype(F32)
            s2[k][f, :] = total
            z_send[k][f, :] = total.astype(BF)

        strips(128, 16, strip)
        z_moves[k] = [
            send(z_send[k].at[pl.ds(pl.multiple_of(((zh + d) % 4) * 32, 32), 32)], z_recv[k].at[d - 1], at_z(d))
            for d in (2, 1, 3)
        ]

    def z_sum(k, columns):
        own = pl.ds(pl.multiple_of(zh * 32, 32), 32)
        return (
            s2[k][own, columns]
            + z_recv[k][0, :, columns].astype(F32)
            + z_recv[k][1, :, columns].astype(F32)
            + z_recv[k][2, :, columns].astype(F32)
        )

    def rotated(values):
        return values * cosv[...] + pltpu.roll(values, 64, 1) * sinv[...]

    kv_moves = {}
    block_rows = pl.multiple_of(g * 512 + y * 128, 128)
    half_rows = pl.multiple_of(g * 512, 512)

    def kv_finish():
        for copy in z_moves[0]:
            copy.wait_recv()
        squares = jnp.sum(z_sum(0, pl.ds(256, 128)), axis=1, keepdims=True)
        scale = lax.rsqrt(squares / D + 1e-05)
        rs_scale[...] = jnp.broadcast_to(scale, (32, 128))
        l_cos.wait()
        l_sin.wait()
        rows = pl.ds(own_row, 32)
        kv[rows, pl.ds(0, HD)] = rotated(z_sum(0, pl.ds(0, HD)) * scale).astype(BF)
        kv[rows, pl.ds(HD, HD)] = (z_sum(0, pl.ds(HD, HD)) * scale).astype(BF)
        kv_moves["z"] = [send(kv.at[rows], kv.at[rows], at_z(d)) for d in (2, 1, 3)]

    def kv_y():
        for copy in kv_moves["z"]:
            copy.wait_recv()
        rows = pl.ds(block_rows, 128)
        kv_moves["y"] = [send(kv.at[rows], kv.at[rows], at_y(d)) for d in (2, 1, 3)]

    def kv_sib():
        for copy in kv_moves["y"]:
            copy.wait_recv()
        rows = pl.ds(half_rows, 512)
        kv_moves["s"] = send(kv.at[rows], kv.at[rows], sibling)

    att_moves = [{}, {}]

    def queries(k):
        for copy in z_moves[k]:
            copy.wait_recv()
        for h in range(8):
            value = z_sum(k, pl.ds(h * HD, HD)) * rs_scale[...]
            qs[k - 1, pl.ds(h * 32, 32), :] = rotated(value).astype(BF)

    def attention(k):
        n = 128
        for part in range(256 // n):
            scores = lax.dot_general(
                qs[k - 1, pl.ds(part * n, n), :], kv[:, pl.ds(0, HD)], (((1,), (1,)), ((), ())), preferred_element_type=F32
            ) * (1.0 / math.sqrt(HD))
            q_pos = own_row + lax.broadcasted_iota(jnp.int32, (n, LEN), 0) % 32
            k_pos = lax.broadcasted_iota(jnp.int32, (n, LEN), 1)
            scores = jnp.where(k_pos <= q_pos, scores, F32(-1e30))
            peak = jnp.max(scores, axis=1, keepdims=True)
            e = jnp.exp(scores - peak)
            probs = (e / jnp.sum(e, axis=1, keepdims=True)).astype(BF)
            value = jnp.dot(probs, kv[:, pl.ds(HD, HD)], preferred_element_type=F32).astype(BF)
            for h in range(n // 32):
                att[k - 1][pl.ds(own_row, 32), pl.ds((part * (n // 32) + h) * HD, HD)] = value[h * 32 : (h + 1) * 32, :]
        rows = pl.ds(own_row, 32)
        att_moves[k - 1]["z"] = [send(att[k - 1].at[rows], att[k - 1].at[rows], at_z(d)) for d in (2, 1, 3)]

    def rows_of(dg, dy, start=0, size=128):
        gg = (g + dg) % 2
        return pl.ds(pl.multiple_of(gg * 512 + ((y + dy) % 4) * 128 + start, 64), size)

    def att_y(a):
        m = att_moves[a]
        for copy in m["z"]:
            copy.wait_recv()
        rows = rows_of(0, 0)
        m["p"] = send(att[a].at[rows], att[a].at[rows], at_y(1))
        m["m"] = send(att[a].at[rows], att[a].at[rows], at_y(3))
        m["s0"] = send(att[a].at[rows], att[a].at[rows], sibling)

    def att_relay(a):
        m = att_moves[a]
        m["p"].wait_recv()
        rows = rows_of(0, 3, 0, 64)
        m["rp"] = send(att[a].at[rows], att[a].at[rows], at_y(1))
        m["m"].wait_recv()
        rows = rows_of(0, 1, 64, 64)
        m["rm"] = send(att[a].at[rows], att[a].at[rows], at_y(3))
        for name, d in (("s3", 3), ("s1", 1)):
            rows = rows_of(0, d)
            m[name] = send(att[a].at[rows], att[a].at[rows], sibling)

    def att_last(a):
        m = att_moves[a]
        m["rp"].wait_recv()
        m["rm"].wait_recv()
        rows = rows_of(0, 2)
        m["s2"] = send(att[a].at[rows], att[a].at[rows], sibling)

    def out_block(a, dg, dy):
        if dg == 1:
            att_moves[a][f"s{dy}"].wait_recv()
        rows = rows_of(dg, dy)
        value = jnp.dot(att[a][rows, :], wo[pl.ds(a * QW, QW), :], preferred_element_type=F32)
        if a == 0:
            acc[rows, :] = value
            return
        total = acc[rows, :] + value
        acc[rows, :] = total
        bsend[rows, :] = total.astype(BF)
        block = ((g + dg) % 2) * 4 + (y + dy) % 4
        index = len(branch_moves)
        copy = pltpu.make_async_remote_copy(
            src_ref=bsend.at[rows],
            dst_ref=brecv.at[c],
            send_sem=bssem.at[index],
            recv_sem=brsem.at[c],
            device_id={"col": block},
            device_id_type=MESH,
        )
        branch_moves.append((block, copy))

        @pl.when(block != c)
        def _():
            copy.start()

    branch_moves = []

    l_k.wait()
    l_v.wait()
    sib_stage(0)
    own_stage(0)
    l_q.wait()
    sib_stage(1)
    y_first(0)
    own_stage(1)
    y_second(0)
    y_first(1)
    sib_stage(2)
    z_first(0)
    y_second(1)
    own_stage(2)
    y_first(2)
    kv_finish()
    z_first(1)
    y_second(2)
    kv_y()
    queries(1)
    kv_sib()
    z_first(2)
    kv_moves["s"].wait_recv()
    attention(1)
    queries(2)
    attention(2)
    att_y(0)
    att_y(1)
    att_relay(0)
    l_o.wait()
    out_block(0, 0, 0)
    out_block(0, 1, 0)
    att_relay(1)
    att_last(0)
    out_block(0, 0, 1)
    out_block(0, 0, 3)
    out_block(0, 1, 1)
    out_block(0, 1, 3)
    out_block(1, 0, 0)
    out_block(1, 1, 0)
    out_block(0, 0, 2)
    out_block(0, 1, 2)
    out_block(1, 0, 1)
    out_block(1, 0, 3)
    out_block(1, 1, 1)
    out_block(1, 1, 3)
    att_last(1)
    out_block(1, 0, 2)
    out_block(1, 1, 2)

    upper, lower = pl.ds(0, 512), pl.ds(512, 512)
    moves_b = []
    for j in range(4):
        block = (zh - j + 4) % 4
        up = describe(panel.at[block, upper], panel.at[block, upper], at_y(1))
        down = describe(panel.at[block, lower], panel.at[block, lower], at_y(3))
        over = describe(panel.at[block], panel.at[block], sibling)
        moves_b.append((block, up, down, over))

    def panel_block(j):
        _, up, down, over = moves_b[j]

        @pl.when(is_source)
        def _():
            if j == 0:
                own_panel.wait()
            else:
                part_a[j - 1].wait_recv()

        @pl.when(jnp.logical_and(panel_core, delta != 0))
        def _():
            up.wait_recv()

        @pl.when(jnp.logical_and(panel_core, delta != 3))
        def _():
            up.start()

        @pl.when(jnp.logical_and(panel_core, delta != 0))
        def _():
            down.wait_recv()

        @pl.when(jnp.logical_and(panel_core, delta != 1))
        def _():
            down.start()

        @pl.when(panel_core)
        def _():
            over.start()

    def panel_end():
        for j, (block, up, down, over) in enumerate(moves_b):
            @pl.when(jnp.logical_and(panel_core, delta != 3))
            def _():
                up.wait_send()

            @pl.when(jnp.logical_and(panel_core, delta != 1))
            def _():
                down.wait_send()

            @pl.when(panel_core)
            def _():
                over.wait_send()

            @pl.when(jnp.logical_not(panel_core))
            def _():
                over.wait_recv()

        @pl.when(is_source)
        def _():
            for copy in part_a:
                copy.wait_send()

    panel_block(0)
    panel_block(1)

    for s in range(1, 8):
        src = (c + s) % 8
        pltpu.make_async_remote_copy(
            src_ref=bsend.at[pl.ds(0, 128)],
            dst_ref=brecv.at[src],
            send_sem=bssem.at[0],
            recv_sem=brsem.at[src],
            device_id={"col": src},
            device_id_type=MESH,
        ).wait_recv()

    def reduce_strip(i):
        r = pl.ds(pl.multiple_of(c * 128 + i, 16), 16)
        total = acc[r, :]
        for s in range(1, 8):
            total = total + brecv[(c + s) % 8, pl.ds(i, 16), :].astype(F32)
        ball[r, :] = total.astype(BF)

    strips(128, 16, reduce_strip)
    last = [send(ball.at[my_tokens], ball.at[my_tokens], at_col(*o)) for o in reversed(col_offsets)]
    panel_block(2)
    panel_block(3)
    for copy in last:
        copy.wait_recv()
    out_branch = pltpu.make_async_copy(ball, branch_out, lsem.at[len(local)])
    local.append(None)
    out_branch.start()
    panel_end()
    out_panel = pltpu.make_async_copy(panel, panel_out, lsem.at[len(local)])
    local.append(None)
    out_panel.start()
    for copy in sends:
        copy.wait_send()
    for block, copy in branch_moves:
        @pl.when(block != c)
        def _():
            copy.wait_send()

    out_tf.wait()
    out_branch.wait()
    out_panel.wait()


def scratch_shapes():
    v = pltpu.VMEM
    shapes = [
        v((LEN, FB), BF),
        v((LEN, FB), BF),
        v((LEN, 128), F32),
        v((FB, 256), BF),
        v((FB, 2 * QW), BF),
        v((2 * QW, FB), BF),
        v((32, 128), F32),
        v((32, 128), F32),
    ]
    shapes += [v((512, w), BF) for w in WIDTHS]
    shapes += [v((512, w), BF) for w in WIDTHS]
    shapes += [v((512, w), F32) for w in WIDTHS]
    for _ in range(6):
        shapes += [v((128, w), BF) for w in WIDTHS]
    shapes += [v((128, w), F32) for w in WIDTHS]
    shapes += [v((128, w), BF) for w in WIDTHS]
    shapes += [v((3, 32, w), BF) for w in WIDTHS]
    shapes += [v((LEN, 256), BF), v((32, 128), F32), v((2, 256, HD), BF)]
    shapes += [v((LEN, QW), BF)] * 2
    shapes += [v((LEN, FB), F32), v((LEN, FB), BF), v((8, 128, FB), BF), v((LEN, FB), BF), v((4, LEN, FB), BF)]
    dma = pltpu.SemaphoreType.DMA
    shapes += [dma((128,)), dma((128,)), dma((16,)), dma((8,)), dma((8,))]
    return shapes


def panel_product(left, right):
    return lax.dot_general(left, right, (((1,), (0,)), ((), ())), preferred_element_type=F32)


def per_device(tokens, norm_gain, query_weight, key_weight, value_weight, output_weight):
    cosine, sine = tables()
    anywhere = pl.BlockSpec(memory_space=pl.ANY)
    in_vmem = pl.BlockSpec(memory_space=pltpu.VMEM)
    gathered, panel, branch = pl.pallas_call(
        kernel,
        out_shape=(
            jax.ShapeDtypeStruct((LEN, FB), BF),
            jax.ShapeDtypeStruct((4, LEN, FB), BF),
            jax.ShapeDtypeStruct((LEN, FB), BF),
        ),
        in_specs=[anywhere, in_vmem] + [anywhere] * 6,
        out_specs=(anywhere,) * 3,
        scratch_shapes=scratch_shapes(),
        compiler_params=pltpu.CompilerParams(
            collective_id=0, has_side_effects=True, vmem_limit_bytes=58 * 2**20
        ),
        name="layer",
    )(
        tokens,
        norm_gain.reshape(1, FB),
        key_weight,
        value_weight,
        query_weight,
        output_weight,
        jnp.asarray(cosine),
        jnp.asarray(sine),
    )
    gram = panel_product(panel, gathered).reshape(4 * FB, FB) / LEN
    cross = panel_product(panel, branch).reshape(4 * FB, FB) / LEN
    return (gram, cross)


def solution(mesh):
    return jax.shard_map(
        per_device,
        mesh=mesh,
        in_specs=(
            P("col", ("grp", "row")),
            P(("grp", "row")),
            P(("grp", "row"), "col"),
            P(("grp", "row"), "col"),
            P(("grp", "row"), "col"),
            P("col", ("grp", "row")),
        ),
        out_specs=(P("col", ("grp", "row")), P("col", ("grp", "row"))),
        check_vma=False,
    )
```

```python
import functools
import math

import jax
import jax.numpy as jnp
import numpy as np
from jax import lax
from jax.experimental import pallas as pl
from jax.experimental.pallas import tpu as pltpu
from jax.sharding import PartitionSpec as P

D = 16384
H = 128
HD = 128
LEN = 1024
MESH = pl.DeviceIdType.MESH
BF = jnp.bfloat16
F32 = jnp.float32
FB = 512
KVW = 384
QW = 1024
WIDTHS = (KVW, QW, QW)


def tables():
    half = HD // 2
    frequency = np.float32(500000.0) ** (-np.arange(half, dtype=np.float32) * np.float32(2.0 / HD))
    angles = np.arange(LEN, dtype=np.float32)[:, None] * frequency.astype(np.float32)[None, :]
    cosine = np.cos(angles.astype(np.float64)).astype(np.float32)
    sine = np.sin(angles.astype(np.float64)).astype(np.float32)
    return (
        np.concatenate([cosine, cosine], axis=1),
        np.concatenate([-sine, sine], axis=1),
    )


def strips(rows, step, body):
    def one(i, carry):
        body(pl.multiple_of(i * step, step))
        return carry

    lax.fori_loop(0, rows // step, one, 0)


class Move:
    def __init__(self, copy):
        self.copy, self.open = copy, True

    def start(self):
        self.copy.start()

    def wait_recv(self):
        self.open = False
        self.copy.wait_recv()

    def wait_send(self):
        self.copy.wait_send()


def kernel(tok, gain, wk_in, wv_in, wq_in, wo_in, cos_in, sin_in, tf_out, panel_out, branch_out, *scratch):
    names = iter(scratch)
    nxt = lambda: next(names)
    tf, xg, sq, wkv, wq, wo, cosv, sinv = [nxt() for _ in range(8)]
    sib_send = [nxt() for _ in range(3)]
    sib_recv = [nxt() for _ in range(3)]
    r1 = [nxt() for _ in range(3)]
    y_send_p = [nxt() for _ in range(3)]
    y_send_m = [nxt() for _ in range(3)]
    y_send_f = [nxt() for _ in range(3)]
    y_recv_p = [nxt() for _ in range(3)]
    y_recv_m = [nxt() for _ in range(3)]
    y_recv_f = [nxt() for _ in range(3)]
    s2 = [nxt() for _ in range(3)]
    z_send = [nxt() for _ in range(3)]
    z_recv = [nxt() for _ in range(3)]
    kv, rs_scale, qs = [nxt() for _ in range(3)]
    att = [nxt() for _ in range(2)]
    acc, bsend, brecv, ball, panel = [nxt() for _ in range(5)]
    ssem, rsem, lsem, bssem, brsem = [nxt() for _ in range(5)]

    g = lax.axis_index("grp")
    row = lax.axis_index("row")
    c = lax.axis_index("col")
    y, zh = row // 4, row % 4
    x, zl = c // 2, c % 2

    def at_y(d):
        return {"row": ((y + d) % 4) * 4 + zh}

    def at_z(d):
        return {"row": y * 4 + (zh + d) % 4}

    def at_col(dx, dl):
        return {"col": ((x + dx) % 4) * 2 + (zl + dl) % 2}

    sibling = {"grp": 1 - g}
    col_offsets = [(0, 1), (1, 0), (3, 0), (1, 1), (3, 1), (2, 0), (2, 1)]

    local = []

    def load(src, dst):
        copy = pltpu.make_async_copy(src, dst, lsem.at[len(local)])
        copy.start()
        local.append(copy)
        return copy

    own_row = pl.multiple_of(g * 512 + y * 128 + zh * 32, 32)
    my_tokens = pl.ds(pl.multiple_of(c * 128, 128), 128)
    l_tok = load(tok, tf.at[my_tokens])
    l_k = load(wk_in, wkv.at[:, pl.ds(0, HD)])
    l_v = load(wv_in, wkv.at[:, pl.ds(HD, HD)])
    l_q = load(wq_in, wq)
    l_cos = load(cos_in.at[pl.ds(own_row, 32)], cosv)
    l_sin = load(sin_in.at[pl.ds(own_row, 32)], sinv)
    l_o = load(wo_in, wo)

    barrier = pltpu.get_barrier_semaphore()
    peers = [sibling] + [at_y(d) for d in (1, 2, 3)] + [at_z(d) for d in (1, 2, 3)]
    peers += [at_col(*o) for o in col_offsets]
    for peer in peers:
        pl.semaphore_signal(barrier, inc=1, device_id=peer, device_id_type=MESH)
    pl.semaphore_wait(barrier, len(peers))

    sends = []
    count = [0]

    def describe(src, dst, dev, index=None):
        if index is None:
            index = count[0]
            count[0] += 1
        return pltpu.make_async_remote_copy(
            src_ref=src,
            dst_ref=dst,
            send_sem=ssem.at[index],
            recv_sem=rsem.at[index],
            device_id=dev,
            device_id_type=MESH,
        )

    def send(src, dst, dev):
        copy = Move(describe(src, dst, dev))
        copy.start()
        sends.append(copy)
        return copy

    gather = [send(tok, tf.at[my_tokens], at_col(*o)) for o in col_offsets]
    l_tok.wait()
    for copy in gather:
        copy.wait_recv()

    panel_core = g == c // 4
    delta = (y - c % 4 + 4) % 4
    is_source = jnp.logical_and(panel_core, delta == 0)

    def quarter(d):
        return pl.ds(pl.multiple_of(((y + d) % 4) * 256, 256), 256)

    spread = [describe(tf.at[quarter(d)], panel.at[zh, quarter(d)], at_y(d)) for d in (1, 2, 3)]
    across = [describe(panel.at[zh, quarter(0)], panel.at[zh, quarter(0)], at_z(d)) for d in (1, 2, 3)]
    pairs = [pl.ds(0, 2), pl.ds(2, 2)]
    along = [
        [describe(panel.at[p, quarter(0)], panel.at[p, quarter(0)], at_y(d)) for d in (1, 3, 2)] for p in pairs
    ]
    over_own = describe(panel.at[:, quarter(0)], panel.at[:, quarter(0)], sibling)
    over = [
        [describe(panel.at[p, quarter(4 - d)], panel.at[p, quarter(4 - d)], sibling) for d in (1, 3, 2)] for p in pairs
    ]
    own_quarter = pltpu.make_async_copy(tf.at[quarter(0)], panel.at[zh, quarter(0)], lsem.at[len(local)])
    local.append(None)

    @pl.when(is_source)
    def _():
        for copy in spread:
            copy.start()
        own_quarter.start()

    def panel_across():
        @pl.when(is_source)
        def _():
            own_quarter.wait()

        for d in (1, 2, 3):
            @pl.when(jnp.logical_and(panel_core, delta == d))
            def _():
                spread[d - 1].wait_recv()

        @pl.when(panel_core)
        def _():
            for copy in across:
                copy.start()

    def panel_along(p):
        @pl.when(panel_core)
        def _():
            if p == 0:
                for copy in across:
                    copy.wait_recv()
                over_own.start()
            for copy in along[p]:
                copy.start()

    def panel_over(p):
        @pl.when(panel_core)
        def _():
            for copy, onward in zip(along[p], over[p]):
                copy.wait_recv()
                onward.start()

    def panel_end():
        @pl.when(is_source)
        def _():
            for copy in spread:
                copy.wait_send()

        @pl.when(panel_core)
        def _():
            for copy in across + along[0] + along[1] + [over_own] + over[0] + over[1]:
                copy.wait_send()

        @pl.when(jnp.logical_not(panel_core))
        def _():
            for copy in [over_own] + over[0] + over[1]:
                copy.wait_recv()

    out_tf = pltpu.make_async_copy(tf, tf_out, lsem.at[len(local)])
    local.append(None)
    out_tf.start()

    def prepare(i):
        rows = pl.ds(i, 32)
        wide = tf[rows, :].astype(F32)
        xg[rows, :] = (wide * gain[...].astype(F32)).astype(BF)
        square = wide * wide
        sq[rows, :] = square[:, 0:128] + square[:, 128:256] + square[:, 256:384] + square[:, 384:512]

    strips(LEN, 32, prepare)

    mine = pl.multiple_of(g * 512, 512)
    theirs = pl.multiple_of((1 - g) * 512, 512)

    def project(k, base, out):
        weights, first, wide = (wkv, 0, 256) if k == 0 else (wq, (k - 1) * QW, QW)

        def tile(i):
            value = jnp.dot(
                xg[pl.ds(base, 512), :],
                weights[:, pl.ds(pl.multiple_of(first + i, 256), 256)],
                preferred_element_type=F32,
            )
            out[:, pl.ds(i, 256)] = value.astype(out.dtype)

        strips(wide, 256, tile)
        if k == 0:
            out[:, pl.ds(256, 128)] = sq[pl.ds(base, 512), :].astype(out.dtype)

    sib = [None] * 3

    def sib_stage(k):
        project(k, theirs, sib_send[k])
        sib[k] = send(sib_send[k], sib_recv[k], sibling)

    def own_stage(k):
        project(k, mine, r1[k])

    def y_rows(d):
        return pl.multiple_of(((y + d) % 4) * 128, 128)

    y_moves = [None] * 3

    def y_first(k):
        sib[k].wait_recv()

        def pair(d, dst, start, rows):
            base = y_rows(d)

            def strip(i):
                r = pl.ds(pl.multiple_of(base + start + i, 16), 16)
                dst[pl.ds(pl.multiple_of(start + i, 16), 16), :] = (r1[k][r, :] + sib_recv[k][r, :].astype(F32)).astype(BF)

            strips(rows, 16, strip)

        top, low = pl.ds(0, 64), pl.ds(64, 64)
        pair(2, y_send_f[k], 0, 128)
        m1p = send(y_send_f[k].at[top], y_recv_f[k].at[top], at_y(1))
        m1m = send(y_send_f[k].at[low], y_recv_f[k].at[low], at_y(3))
        pair(1, y_send_p[k], 64, 64)
        m2p = send(y_send_p[k].at[low], y_recv_p[k].at[low], at_y(1))
        pair(3, y_send_m[k], 0, 64)
        m2m = send(y_send_m[k].at[top], y_recv_m[k].at[top], at_y(3))
        y_moves[k] = [m1p, m1m, m2p, m2m]

    def y_second(k):
        top, low = pl.ds(0, 64), pl.ds(64, 64)
        m1p, m1m = y_moves[k][:2]

        def relay(d, dst, start):
            base = y_rows(d)

            def strip(i):
                r = pl.ds(pl.multiple_of(base + start + i, 16), 16)
                f = pl.ds(pl.multiple_of(start + i, 16), 16)
                dst[f, :] = (r1[k][r, :] + sib_recv[k][r, :].astype(F32) + y_recv_f[k][f, :].astype(F32)).astype(BF)

            strips(64, 16, strip)

        m1p.wait_recv()
        relay(1, y_send_p[k], 0)
        m3p = send(y_send_p[k].at[top], y_recv_p[k].at[top], at_y(1))
        m1m.wait_recv()
        relay(3, y_send_m[k], 64)
        m3m = send(y_send_m[k].at[low], y_recv_m[k].at[low], at_y(3))
        y_moves[k] += [m3p, m3m]

    z_moves = [None] * 3

    def z_first(k):
        for copy in y_moves[k][2:]:
            copy.wait_recv()
        base = y_rows(0)

        def strip(i):
            r = pl.ds(pl.multiple_of(base + i, 16), 16)
            f = pl.ds(i, 16)
            total = r1[k][r, :] + sib_recv[k][r, :].astype(F32) + y_recv_p[k][f, :].astype(F32) + y_recv_m[k][f, :].astype(F32)
            s2[k][f, :] = total
            z_send[k][f, :] = total.astype(BF)

        strips(128, 16, strip)
        z_moves[k] = [
            send(z_send[k].at[pl.ds(pl.multiple_of(((zh + d) % 4) * 32, 32), 32)], z_recv[k].at[d - 1], at_z(d))
            for d in (2, 1, 3)
        ]

    def z_sum(k, columns):
        own = pl.ds(pl.multiple_of(zh * 32, 32), 32)
        return (
            s2[k][own, columns]
            + z_recv[k][0, :, columns].astype(F32)
            + z_recv[k][1, :, columns].astype(F32)
            + z_recv[k][2, :, columns].astype(F32)
        )

    def rotated(values):
        return values * cosv[...] + pltpu.roll(values, 64, 1) * sinv[...]

    kv_moves = {}
    block_rows = pl.multiple_of(g * 512 + y * 128, 128)
    half_rows = pl.multiple_of(g * 512, 512)

    def kv_finish():
        for copy in z_moves[0]:
            copy.wait_recv()
        squares = jnp.sum(z_sum(0, pl.ds(256, 128)), axis=1, keepdims=True)
        scale = lax.rsqrt(squares / D + 1e-05)
        rs_scale[...] = jnp.broadcast_to(scale, (32, 128))
        l_cos.wait()
        l_sin.wait()
        rows = pl.ds(own_row, 32)
        kv[rows, pl.ds(0, HD)] = rotated(z_sum(0, pl.ds(0, HD)) * scale).astype(BF)
        kv[rows, pl.ds(HD, HD)] = (z_sum(0, pl.ds(HD, HD)) * scale).astype(BF)
        kv_moves["z"] = [send(kv.at[rows], kv.at[rows], at_z(d)) for d in (2, 1, 3)]

    def kv_y():
        for copy in kv_moves["z"]:
            copy.wait_recv()
        rows = pl.ds(block_rows, 128)
        kv_moves["y"] = [send(kv.at[rows], kv.at[rows], at_y(d)) for d in (2, 1, 3)]

    def kv_sib():
        for copy in kv_moves["y"]:
            copy.wait_recv()
        rows = pl.ds(half_rows, 512)
        kv_moves["s"] = send(kv.at[rows], kv.at[rows], sibling)

    def kv_here():
        kv_moves["s"].wait_recv()

    att_moves = [{}, {}]

    def queries(k):
        for copy in z_moves[k]:
            copy.wait_recv()
        for h in range(8):
            value = z_sum(k, pl.ds(h * HD, HD)) * rs_scale[...]
            qs[k - 1, pl.ds(h * 32, 32), :] = rotated(value).astype(BF)

    def attention(k):
        n = 128
        for part in range(256 // n):
            scores = lax.dot_general(
                qs[k - 1, pl.ds(part * n, n), :], kv[:, pl.ds(0, HD)], (((1,), (1,)), ((), ())), preferred_element_type=F32
            ) * (1.0 / math.sqrt(HD))
            q_pos = own_row + lax.broadcasted_iota(jnp.int32, (n, LEN), 0) % 32
            k_pos = lax.broadcasted_iota(jnp.int32, (n, LEN), 1)
            scores = jnp.where(k_pos <= q_pos, scores, F32(-1e30))
            peak = jnp.max(scores, axis=1, keepdims=True)
            e = jnp.exp(scores - peak)
            probs = (e / jnp.sum(e, axis=1, keepdims=True)).astype(BF)
            value = jnp.dot(probs, kv[:, pl.ds(HD, HD)], preferred_element_type=F32).astype(BF)
            for h in range(n // 32):
                att[k - 1][pl.ds(own_row, 32), pl.ds((part * (n // 32) + h) * HD, HD)] = value[h * 32 : (h + 1) * 32, :]
        rows = pl.ds(own_row, 32)
        att_moves[k - 1]["z"] = [send(att[k - 1].at[rows], att[k - 1].at[rows], at_z(d)) for d in (2, 1, 3)]

    def rows_of(dg, dy, start=0, size=128):
        gg = (g + dg) % 2
        return pl.ds(pl.multiple_of(gg * 512 + ((y + dy) % 4) * 128 + start, 64), size)

    def att_y(a):
        m = att_moves[a]
        for copy in m["z"]:
            copy.wait_recv()
        rows = rows_of(0, 0)
        m["p"] = send(att[a].at[rows], att[a].at[rows], at_y(1))
        m["m"] = send(att[a].at[rows], att[a].at[rows], at_y(3))
        m["s0"] = send(att[a].at[rows], att[a].at[rows], sibling)

    def att_relay(a):
        m = att_moves[a]
        m["p"].wait_recv()
        rows = rows_of(0, 3, 0, 64)
        m["rp"] = send(att[a].at[rows], att[a].at[rows], at_y(1))
        m["m"].wait_recv()
        rows = rows_of(0, 1, 64, 64)
        m["rm"] = send(att[a].at[rows], att[a].at[rows], at_y(3))
        for name, d in (("s3", 3), ("s1", 1)):
            rows = rows_of(0, d)
            m[name] = send(att[a].at[rows], att[a].at[rows], sibling)

    def att_last(a):
        m = att_moves[a]
        m["rp"].wait_recv()
        m["rm"].wait_recv()
        rows = rows_of(0, 2)
        m["s2"] = send(att[a].at[rows], att[a].at[rows], sibling)

    def out_block(a, dg, dy):
        if dg == 1:
            att_moves[a][f"s{dy}"].wait_recv()
        rows = rows_of(dg, dy)
        value = jnp.dot(att[a][rows, :], wo[pl.ds(a * QW, QW), :], preferred_element_type=F32)
        if a == 0:
            acc[rows, :] = value
            return
        total = acc[rows, :] + value
        acc[rows, :] = total
        bsend[rows, :] = total.astype(BF)
        block = ((g + dg) % 2) * 4 + (y + dy) % 4
        index = len(branch_moves)
        copy = pltpu.make_async_remote_copy(
            src_ref=bsend.at[rows],
            dst_ref=brecv.at[c],
            send_sem=bssem.at[index],
            recv_sem=brsem.at[c],
            device_id={"col": block},
            device_id_type=MESH,
        )
        branch_moves.append((block, copy))

        @pl.when(block != c)
        def _():
            copy.start()

    branch_moves = []

    def branch_sum():
        for s in range(1, 8):
            src = (c + s) % 8
            pltpu.make_async_remote_copy(
                src_ref=bsend.at[pl.ds(0, 128)],
                dst_ref=brecv.at[src],
                send_sem=bssem.at[0],
                recv_sem=brsem.at[src],
                device_id={"col": src},
                device_id_type=MESH,
            ).wait_recv()

        def reduce_strip(i):
            r = pl.ds(pl.multiple_of(c * 128 + i, 16), 16)
            total = acc[r, :]
            for s in range(1, 8):
                total = total + brecv[(c + s) % 8, pl.ds(i, 16), :].astype(F32)
            ball[r, :] = total.astype(BF)

        strips(128, 16, reduce_strip)
        last = [send(ball.at[my_tokens], ball.at[my_tokens], at_col(*o)) for o in reversed(col_offsets)]
        branch_last.extend(last)

    def branch_end():
        for copy in branch_last:
            copy.wait_recv()
        out_branch.start()

    branch_last = []
    out_branch = pltpu.make_async_copy(ball, branch_out, lsem.at[len(local)])
    local.append(None)
    out_panel = pltpu.make_async_copy(panel, panel_out, lsem.at[len(local)])
    local.append(None)

    def loaded(*copies):
        for copy in copies:
            copy.wait()

    plan = [
        (loaded, l_k, l_v),
        (sib_stage, 0),
        (own_stage, 0),
        (loaded, l_q),
        (sib_stage, 1),
        (y_first, 0),
        (own_stage, 1),
        (panel_across,),
        (y_second, 0),
        (y_first, 1),
        (sib_stage, 2),
        (z_first, 0),
        (y_second, 1),
        (own_stage, 2),
        (y_first, 2),
        (kv_finish,),
        (z_first, 1),
        (y_second, 2),
        (kv_y,),
        (queries, 1),
        (kv_sib,),
        (z_first, 2),
        (kv_here,),
        (panel_along, 0),
        (attention, 1),
        (queries, 2),
        (att_y, 0),
        (attention, 2),
        (att_y, 1),
        (att_relay, 0),
        (loaded, l_o),
        (out_block, 0, 0, 0),
        (out_block, 0, 1, 0),
        (att_relay, 1),
        (att_last, 0),
        (out_block, 0, 0, 1),
        (out_block, 0, 0, 3),
        (out_block, 0, 1, 1),
        (out_block, 0, 1, 3),
        (out_block, 1, 0, 0),
        (out_block, 1, 1, 0),
        (out_block, 0, 0, 2),
        (out_block, 0, 1, 2),
        (out_block, 1, 0, 1),
        (out_block, 1, 0, 3),
        (out_block, 1, 1, 1),
        (out_block, 1, 1, 3),
        (att_last, 1),
        (panel_along, 1),
        (out_block, 1, 0, 2),
        (out_block, 1, 1, 2),
        (branch_sum,),
        (panel_over, 0),
        (panel_over, 1),
        (branch_end,),
        (panel_end,),
    ]
    for stage, *values in plan:
        stage(*values)
    out_panel.start()
    for copy in sends:
        copy.wait_send()
    for block, copy in branch_moves:
        @pl.when(block != c)
        def _():
            copy.wait_send()

    out_tf.wait()
    out_branch.wait()
    out_panel.wait()


def scratch_shapes():
    v = pltpu.VMEM
    shapes = [
        v((LEN, FB), BF),
        v((LEN, FB), BF),
        v((LEN, 128), F32),
        v((FB, 256), BF),
        v((FB, 2 * QW), BF),
        v((2 * QW, FB), BF),
        v((32, 128), F32),
        v((32, 128), F32),
    ]
    shapes += [v((512, w), BF) for w in WIDTHS]
    shapes += [v((512, w), BF) for w in WIDTHS]
    shapes += [v((512, w), F32) for w in WIDTHS]
    for _ in range(6):
        shapes += [v((128, w), BF) for w in WIDTHS]
    shapes += [v((128, w), F32) for w in WIDTHS]
    shapes += [v((128, w), BF) for w in WIDTHS]
    shapes += [v((3, 32, w), BF) for w in WIDTHS]
    shapes += [v((LEN, 256), BF), v((32, 128), F32), v((2, 256, HD), BF)]
    shapes += [v((LEN, QW), BF)] * 2
    shapes += [v((LEN, FB), F32), v((LEN, FB), BF), v((8, 128, FB), BF), v((LEN, FB), BF), v((4, LEN, FB), BF)]
    dma = pltpu.SemaphoreType.DMA
    shapes += [dma((128,)), dma((128,)), dma((16,)), dma((8,)), dma((8,))]
    return shapes


def panel_product(left, right):
    return lax.dot_general(left, right, (((1,), (0,)), ((), ())), preferred_element_type=F32)


def per_device(tokens, norm_gain, query_weight, key_weight, value_weight, output_weight):
    cosine, sine = tables()
    anywhere = pl.BlockSpec(memory_space=pl.ANY)
    in_vmem = pl.BlockSpec(memory_space=pltpu.VMEM)
    gathered, panel, branch = pl.pallas_call(
        kernel,
        out_shape=(
            jax.ShapeDtypeStruct((LEN, FB), BF),
            jax.ShapeDtypeStruct((4, LEN, FB), BF),
            jax.ShapeDtypeStruct((LEN, FB), BF),
        ),
        in_specs=[anywhere, in_vmem] + [anywhere] * 6,
        out_specs=(anywhere,) * 3,
        scratch_shapes=scratch_shapes(),
        compiler_params=pltpu.CompilerParams(
            collective_id=0, has_side_effects=True, vmem_limit_bytes=58 * 2**20
        ),
        name="layer",
    )(
        tokens,
        norm_gain.reshape(1, FB),
        key_weight,
        value_weight,
        query_weight,
        output_weight,
        jnp.asarray(cosine),
        jnp.asarray(sine),
    )
    gram = panel_product(panel, gathered).reshape(4 * FB, FB) / LEN
    cross = panel_product(panel, branch).reshape(4 * FB, FB) / LEN
    return (gram, cross)


def solution(mesh):
    return jax.shard_map(
        per_device,
        mesh=mesh,
        in_specs=(
            P("col", ("grp", "row")),
            P(("grp", "row")),
            P(("grp", "row"), "col"),
            P(("grp", "row"), "col"),
            P(("grp", "row"), "col"),
            P("col", ("grp", "row")),
        ),
        out_specs=(P("col", ("grp", "row")), P("col", ("grp", "row"))),
        check_vma=False,
    )
```

```python
import functools
import math

import jax
import jax.numpy as jnp
import numpy as np
from jax import lax
from jax.experimental import pallas as pl
from jax.experimental.pallas import tpu as pltpu
from jax.sharding import PartitionSpec as P

D = 16384
H = 128
HD = 128
LEN = 1024
MESH = pl.DeviceIdType.MESH
BF = jnp.bfloat16
F32 = jnp.float32
FB = 512
KVW = 384
QW = 1024
WIDTHS = (KVW, QW, QW)


def tables():
    half = HD // 2
    frequency = np.float32(500000.0) ** (-np.arange(half, dtype=np.float32) * np.float32(2.0 / HD))
    angles = np.arange(LEN, dtype=np.float32)[:, None] * frequency.astype(np.float32)[None, :]
    cosine = np.cos(angles.astype(np.float64)).astype(np.float32)
    sine = np.sin(angles.astype(np.float64)).astype(np.float32)
    return (
        np.concatenate([cosine, cosine], axis=1),
        np.concatenate([-sine, sine], axis=1),
    )


def strips(rows, step, body):
    def one(i, carry):
        body(pl.multiple_of(i * step, step))
        return carry

    lax.fori_loop(0, rows // step, one, 0)


class Move:
    def __init__(self, copy):
        self.copy, self.open = copy, True

    def start(self):
        self.copy.start()

    def wait_recv(self):
        self.open = False
        self.copy.wait_recv()

    def wait_send(self):
        self.copy.wait_send()


def kernel(tok, gain, wk_in, wv_in, wq_in, wo_in, cos_in, sin_in, tf_out, panel_out, branch_out, *scratch):
    names = iter(scratch)
    nxt = lambda: next(names)
    tf, xg, sq, wkv, wq, wo, cosv, sinv = [nxt() for _ in range(8)]
    sib_send = [nxt() for _ in range(3)]
    sib_recv = [nxt() for _ in range(3)]
    r1 = [nxt() for _ in range(3)]
    y_send_p = [nxt() for _ in range(3)]
    y_send_m = [nxt() for _ in range(3)]
    y_send_f = [nxt() for _ in range(3)]
    y_recv_p = [nxt() for _ in range(3)]
    y_recv_m = [nxt() for _ in range(3)]
    y_recv_f = [nxt() for _ in range(3)]
    s2 = [nxt() for _ in range(3)]
    z_send = [nxt() for _ in range(3)]
    z_recv = [nxt() for _ in range(3)]
    kv, rs_scale, qs, bias = [nxt() for _ in range(4)]
    att = [nxt() for _ in range(2)]
    acc, bsend, brecv, ball, panel = [nxt() for _ in range(5)]
    ssem, rsem, lsem, bssem, brsem = [nxt() for _ in range(5)]

    g = lax.axis_index("grp")
    row = lax.axis_index("row")
    c = lax.axis_index("col")
    y, zh = row // 4, row % 4
    x, zl = c // 2, c % 2

    def at_y(d):
        return {"row": ((y + d) % 4) * 4 + zh}

    def at_z(d):
        return {"row": y * 4 + (zh + d) % 4}

    def at_col(dx, dl):
        return {"col": ((x + dx) % 4) * 2 + (zl + dl) % 2}

    sibling = {"grp": 1 - g}
    col_offsets = [(0, 1), (1, 0), (3, 0), (1, 1), (3, 1), (2, 0), (2, 1)]

    local = []

    def load(src, dst):
        copy = pltpu.make_async_copy(src, dst, lsem.at[len(local)])
        copy.start()
        local.append(copy)
        return copy

    own_row = pl.multiple_of(g * 512 + y * 128 + zh * 32, 32)
    first_token = pl.multiple_of(((g * 4 + y + c) % 8) * 128 + zh * 32, 32)
    my_tokens = pl.ds(pl.multiple_of(c * 128, 128), 128)
    l_tok = load(tok, tf.at[my_tokens])
    l_k = load(wk_in, wkv.at[:, pl.ds(0, HD)])
    l_v = load(wv_in, wkv.at[:, pl.ds(HD, HD)])
    l_q = load(wq_in, wq)
    l_cos = load(cos_in.at[pl.ds(first_token, 32)], cosv)
    l_sin = load(sin_in.at[pl.ds(first_token, 32)], sinv)
    l_o = load(wo_in, wo)

    barrier = pltpu.get_barrier_semaphore()
    peers = [sibling] + [at_y(d) for d in (1, 2, 3)] + [at_z(d) for d in (1, 2, 3)]
    peers += [at_col(*o) for o in col_offsets]
    for peer in peers:
        pl.semaphore_signal(barrier, inc=1, device_id=peer, device_id_type=MESH)
    pl.semaphore_wait(barrier, len(peers))

    sends = []
    count = [0]

    def describe(src, dst, dev, index=None):
        if index is None:
            index = count[0]
            count[0] += 1
        return pltpu.make_async_remote_copy(
            src_ref=src,
            dst_ref=dst,
            send_sem=ssem.at[index],
            recv_sem=rsem.at[index],
            device_id=dev,
            device_id_type=MESH,
        )

    def send(src, dst, dev):
        copy = Move(describe(src, dst, dev))
        copy.start()
        sends.append(copy)
        return copy

    gather = [send(tok, tf.at[my_tokens], at_col(*o)) for o in col_offsets]
    positions = first_token + lax.broadcasted_iota(jnp.int32, (32, 128), 0)
    for v in range(8):
        keys_at = ((v + c) % 8) * 128 + lax.broadcasted_iota(jnp.int32, (32, 128), 1)
        bias[:, v * 128 : (v + 1) * 128] = jnp.where(keys_at <= positions, F32(0), F32(-1e30))

    panel_core = g == c // 4
    delta = (y - c % 4 + 4) % 4
    is_source = jnp.logical_and(panel_core, delta == 0)

    def quarter(d):
        return pl.ds(pl.multiple_of(((y + d) % 4) * 256, 256), 256)

    spread = [describe(tf.at[quarter(d)], panel.at[zh, quarter(d)], at_y(d)) for d in (1, 2, 3)]
    across = [describe(panel.at[zh, quarter(0)], panel.at[zh, quarter(0)], at_z(d)) for d in (1, 2, 3)]
    along = [describe(panel.at[:, quarter(0)], panel.at[:, quarter(0)], at_y(d)) for d in (1, 3)]
    relays = [
        describe(panel.at[p, quarter(d)], panel.at[p, quarter(d)], at_y(4 - d)) for p, d in ((pl.ds(0, 2), 3), (pl.ds(2, 2), 1))
    ]
    over = [describe(panel.at[:, quarter(d)], panel.at[:, quarter(d)], sibling) for d in (0, 3, 1, 2)]
    own_quarter = pltpu.make_async_copy(tf.at[quarter(0)], panel.at[zh, quarter(0)], lsem.at[len(local)])
    local.append(None)

    def panel_spread():
        out_tf.start()

        @pl.when(is_source)
        def _():
            for copy in spread:
                copy.start()
            own_quarter.start()

    def panel_across():
        @pl.when(is_source)
        def _():
            own_quarter.wait()

        for d in (1, 2, 3):
            @pl.when(jnp.logical_and(panel_core, delta == d))
            def _():
                spread[d - 1].wait_recv()

        @pl.when(panel_core)
        def _():
            for copy in across:
                copy.start()

    def panel_along():
        @pl.when(panel_core)
        def _():
            for copy in across:
                copy.wait_recv()
            for copy in along:
                copy.start()
            over[0].start()

    def panel_relay():
        @pl.when(panel_core)
        def _():
            for i in range(2):
                along[i].wait_recv()
                relays[i].start()
            over[1].start()
            over[2].start()

    def panel_last():
        @pl.when(panel_core)
        def _():
            for copy in relays:
                copy.wait_recv()
            over[3].start()

    def panel_end():
        @pl.when(is_source)
        def _():
            for copy in spread:
                copy.wait_send()

        @pl.when(panel_core)
        def _():
            for copy in across + along + relays + over:
                copy.wait_send()

        @pl.when(jnp.logical_not(panel_core))
        def _():
            for copy in over:
                copy.wait_recv()

    out_tf = pltpu.make_async_copy(tf, tf_out, lsem.at[len(local)])
    local.append(None)

    sib = [[], [], []]

    def arrive(i):
        dx, dl = ((0, 0), *col_offsets)[i]
        if i == 0:
            l_tok.wait()
        else:
            gather[i - 1].wait_recv()
        block = ((x + 4 - dx) % 4) * 2 + (zl + dl) % 2
        base = pl.multiple_of(block * 128, 128)
        slot = (block + 8 - c) % 8
        here = slot // 4 == g
        part = pl.ds(pl.multiple_of((slot % 4) * 128, 128), 128)

        def prepare(j):
            rows = pl.ds(pl.multiple_of(base + j, 32), 32)
            wide = tf[rows, :].astype(F32)
            xg[rows, :] = (wide * gain[...].astype(F32)[None, :]).astype(BF)
            square = wide * wide
            sq[rows, :] = square[:, 0:128] + square[:, 128:256] + square[:, 256:384] + square[:, 384:512]

        strips(128, 32, prepare)

        rows = pl.ds(base, 128)
        for k in range(3):
            def project(out):
                weights = wkv[...] if k == 0 else wq[:, (k - 1) * QW : k * QW]
                wide = weights.shape[1]
                out[part, 0:wide] = jnp.dot(xg[rows, :], weights, preferred_element_type=F32).astype(out.dtype)
                if k == 0:
                    out[part, 256:384] = sq[rows, :].astype(out.dtype)

            @pl.when(here)
            def _():
                project(r1[k])

            @pl.when(jnp.logical_not(here))
            def _():
                project(sib_send[k])

            copy = describe(sib_send[k].at[part], sib_recv[k].at[part], sibling)
            sib[k].append((here, copy))

            @pl.when(jnp.logical_not(here))
            def _():
                copy.start()

    def sib_end():
        for moves in sib:
            for here, copy in moves:
                @pl.when(jnp.logical_not(here))
                def _():
                    copy.wait_send()

    def y_rows(d):
        return pl.multiple_of(((y + d) % 4) * 128, 128)

    y_moves = [None] * 3

    def y_first(k):
        for here, copy in sib[k]:
            @pl.when(here)
            def _():
                copy.wait_recv()


        def pair(d, dst, start, rows):
            base = y_rows(d)

            def strip(i):
                r = pl.ds(pl.multiple_of(base + start + i, 16), 16)
                dst[pl.ds(pl.multiple_of(start + i, 16), 16), :] = (r1[k][r, :] + sib_recv[k][r, :].astype(F32)).astype(BF)

            strips(rows, 16, strip)

        top, low = pl.ds(0, 64), pl.ds(64, 64)
        pair(2, y_send_f[k], 0, 128)
        m1p = send(y_send_f[k].at[top], y_recv_f[k].at[top], at_y(1))
        m1m = send(y_send_f[k].at[low], y_recv_f[k].at[low], at_y(3))
        pair(1, y_send_p[k], 64, 64)
        m2p = send(y_send_p[k].at[low], y_recv_p[k].at[low], at_y(1))
        pair(3, y_send_m[k], 0, 64)
        m2m = send(y_send_m[k].at[top], y_recv_m[k].at[top], at_y(3))
        y_moves[k] = [m1p, m1m, m2p, m2m]

    def y_second(k):
        top, low = pl.ds(0, 64), pl.ds(64, 64)
        m1p, m1m = y_moves[k][:2]

        def relay(d, dst, start):
            base = y_rows(d)

            def strip(i):
                r = pl.ds(pl.multiple_of(base + start + i, 16), 16)
                f = pl.ds(pl.multiple_of(start + i, 16), 16)
                dst[f, :] = (r1[k][r, :] + sib_recv[k][r, :].astype(F32) + y_recv_f[k][f, :].astype(F32)).astype(BF)

            strips(64, 16, strip)

        m1p.wait_recv()
        relay(1, y_send_p[k], 0)
        m3p = send(y_send_p[k].at[top], y_recv_p[k].at[top], at_y(1))
        m1m.wait_recv()
        relay(3, y_send_m[k], 64)
        m3m = send(y_send_m[k].at[low], y_recv_m[k].at[low], at_y(3))
        y_moves[k] += [m3p, m3m]

    z_moves = [None] * 3

    def z_first(k):
        for copy in y_moves[k][2:]:
            copy.wait_recv()
        base = y_rows(0)

        def strip(i):
            r = pl.ds(pl.multiple_of(base + i, 16), 16)
            f = pl.ds(i, 16)
            total = r1[k][r, :] + sib_recv[k][r, :].astype(F32) + y_recv_p[k][f, :].astype(F32) + y_recv_m[k][f, :].astype(F32)
            s2[k][f, :] = total
            z_send[k][f, :] = total.astype(BF)

        strips(128, 16, strip)
        z_moves[k] = [
            send(z_send[k].at[pl.ds(pl.multiple_of(((zh + d) % 4) * 32, 32), 32)], z_recv[k].at[d - 1], at_z(d))
            for d in (2, 1, 3)
        ]

    def z_sum(k, columns):
        own = pl.ds(pl.multiple_of(zh * 32, 32), 32)
        return (
            s2[k][own, columns]
            + z_recv[k][0, :, columns].astype(F32)
            + z_recv[k][1, :, columns].astype(F32)
            + z_recv[k][2, :, columns].astype(F32)
        )

    def rotated(values):
        return values * cosv[...] + pltpu.roll(values, 64, 1) * sinv[...]

    kv_moves = {}
    block_rows = pl.multiple_of(g * 512 + y * 128, 128)
    half_rows = pl.multiple_of(g * 512, 512)

    def kv_finish():
        for copy in z_moves[0]:
            copy.wait_recv()
        squares = jnp.sum(z_sum(0, pl.ds(256, 128)), axis=1, keepdims=True)
        scale = lax.rsqrt(squares / D + 1e-05)
        rs_scale[...] = jnp.broadcast_to(scale, (32, 128))
        l_cos.wait()
        l_sin.wait()
        rows = pl.ds(own_row, 32)
        kv[rows, pl.ds(0, HD)] = rotated(z_sum(0, pl.ds(0, HD)) * scale).astype(BF)
        kv[rows, pl.ds(HD, HD)] = (z_sum(0, pl.ds(HD, HD)) * scale).astype(BF)
        kv_moves["z"] = [send(kv.at[rows], kv.at[rows], at_z(d)) for d in (2, 1, 3)]

    def kv_y():
        for copy in kv_moves["z"]:
            copy.wait_recv()
        rows = pl.ds(block_rows, 128)
        kv_moves["y"] = [send(kv.at[rows], kv.at[rows], at_y(d)) for d in (2, 1, 3)]

    def kv_sib():
        for copy in kv_moves["y"]:
            copy.wait_recv()
        rows = pl.ds(half_rows, 512)
        kv_moves["s"] = send(kv.at[rows], kv.at[rows], sibling)

    def kv_here():
        kv_moves["s"].wait_recv()

    att_moves = [{}, {}]

    def queries(k):
        for copy in z_moves[k]:
            copy.wait_recv()
        for h in range(8):
            value = z_sum(k, pl.ds(h * HD, HD)) * rs_scale[...]
            qs[k - 1, pl.ds(h * 32, 32), :] = rotated(value).astype(BF)

    def attention(k):
        n = 256
        for part in range(256 // n):
            scores = lax.dot_general(
                qs[k - 1, pl.ds(part * n, n), :], kv[:, pl.ds(0, HD)], (((1,), (1,)), ((), ())), preferred_element_type=F32
            ) * (1.0 / math.sqrt(HD))
            scores = (scores.reshape(n // 32, 32, LEN) + bias[...][None]).reshape(n, LEN)
            peak = jnp.max(scores, axis=1, keepdims=True)
            e = jnp.exp(scores - peak)
            probs = (e * (1.0 / jnp.sum(e, axis=1, keepdims=True))).astype(BF)
            value = jnp.dot(probs, kv[:, pl.ds(HD, HD)], preferred_element_type=F32).astype(BF)
            for h in range(n // 32):
                att[k - 1][pl.ds(own_row, 32), pl.ds((part * (n // 32) + h) * HD, HD)] = value[h * 32 : (h + 1) * 32, :]
        rows = pl.ds(own_row, 32)
        att_moves[k - 1]["z"] = [send(att[k - 1].at[rows], att[k - 1].at[rows], at_z(d)) for d in (2, 1, 3)]

    def rows_of(dg, dy, start=0, size=128):
        gg = (g + dg) % 2
        return pl.ds(pl.multiple_of(gg * 512 + ((y + dy) % 4) * 128 + start, 64), size)

    def att_y(a):
        m = att_moves[a]
        for copy in m["z"]:
            copy.wait_recv()
        rows = rows_of(0, 0)
        m["p"] = send(att[a].at[rows], att[a].at[rows], at_y(1))
        m["m"] = send(att[a].at[rows], att[a].at[rows], at_y(3))
        m["s0"] = send(att[a].at[rows], att[a].at[rows], sibling)

    def att_relay(a):
        m = att_moves[a]
        m["p"].wait_recv()
        rows = rows_of(0, 3, 0, 64)
        m["rp"] = send(att[a].at[rows], att[a].at[rows], at_y(1))
        m["m"].wait_recv()
        rows = rows_of(0, 1, 64, 64)
        m["rm"] = send(att[a].at[rows], att[a].at[rows], at_y(3))
        for name, d in (("s3", 3), ("s1", 1)):
            rows = rows_of(0, d)
            m[name] = send(att[a].at[rows], att[a].at[rows], sibling)

    def att_last(a):
        m = att_moves[a]
        m["rp"].wait_recv()
        m["rm"].wait_recv()
        rows = rows_of(0, 2)
        m["s2"] = send(att[a].at[rows], att[a].at[rows], sibling)

    def out_block(a, dg, dy):
        if dg == 1:
            att_moves[a][f"s{dy}"].wait_recv()
        rows = rows_of(dg, dy)
        value = jnp.dot(att[a][rows, :], wo[pl.ds(a * QW, QW), :], preferred_element_type=F32)
        if a == 0:
            acc[rows, :] = value
            return
        total = acc[rows, :] + value
        acc[rows, :] = total
        bsend[rows, :] = total.astype(BF)
        block = ((g + dg) % 2) * 4 + (y + dy) % 4
        index = len(branch_moves)
        copy = pltpu.make_async_remote_copy(
            src_ref=bsend.at[rows],
            dst_ref=brecv.at[c],
            send_sem=bssem.at[index],
            recv_sem=brsem.at[c],
            device_id={"col": (block + c) % 8},
            device_id_type=MESH,
        )
        branch_moves.append((block, copy))

        @pl.when(block != 0)
        def _():
            copy.start()

    branch_moves = []

    def branch_sum():
        for s in range(1, 8):
            src = (c + s) % 8
            pltpu.make_async_remote_copy(
                src_ref=bsend.at[pl.ds(0, 128)],
                dst_ref=brecv.at[src],
                send_sem=bssem.at[0],
                recv_sem=brsem.at[src],
                device_id={"col": src},
                device_id_type=MESH,
            ).wait_recv()

        def reduce_strip(i):
            r = pl.ds(pl.multiple_of(c * 128 + i, 16), 16)
            total = acc[pl.ds(i, 16), :]
            for s in range(1, 8):
                total = total + brecv[(c + s) % 8, pl.ds(i, 16), :].astype(F32)
            ball[r, :] = total.astype(BF)

        strips(128, 16, reduce_strip)
        last = [send(ball.at[my_tokens], ball.at[my_tokens], at_col(*o)) for o in reversed(col_offsets)]
        branch_last.extend(last)

    def branch_end():
        for copy in branch_last:
            copy.wait_recv()
        out_branch.start()

    branch_last = []
    out_branch = pltpu.make_async_copy(ball, branch_out, lsem.at[len(local)])
    local.append(None)
    out_panel = pltpu.make_async_copy(panel, panel_out, lsem.at[len(local)])
    local.append(None)

    def loaded(*copies):
        for copy in copies:
            copy.wait()

    plan = [
        (loaded, l_k, l_v, l_q),
        *[(arrive, i) for i in range(8)],
        (panel_spread,),
        (y_first, 0),
        (y_first, 1),
        (y_second, 0),
        (y_first, 2),
        (z_first, 0),
        (panel_across,),
        (y_second, 1),
        (kv_finish,),
        (z_first, 1),
        (y_second, 2),
        (kv_y,),
        (queries, 1),
        (kv_sib,),
        (z_first, 2),
        (kv_here,),
        (panel_along,),
        (attention, 1),
        (queries, 2),
        (att_y, 0),
        (attention, 2),
        (att_y, 1),
        (loaded, l_o),
        (out_block, 0, 0, 0),
        (out_block, 1, 0, 0),
        (out_block, 0, 1, 0),
        (att_relay, 0),
        (out_block, 1, 1, 0),
        (out_block, 0, 0, 1),
        (out_block, 0, 0, 3),
        (att_relay, 1),
        (out_block, 1, 0, 1),
        (out_block, 1, 0, 3),
        (out_block, 0, 1, 1),
        (out_block, 0, 1, 3),
        (att_last, 0),
        (out_block, 1, 1, 1),
        (out_block, 1, 1, 3),
        (out_block, 0, 0, 2),
        (out_block, 0, 1, 2),
        (att_last, 1),
        (out_block, 1, 0, 2),
        (out_block, 1, 1, 2),
        (panel_relay,),
        (branch_sum,),
        (panel_last,),
        (branch_end,),
        (panel_end,),
        (sib_end,),
    ]
    for stage, *values in plan:
        stage(*values)
    out_panel.start()
    for copy in sends:
        copy.wait_send()
    for block, copy in branch_moves:
        @pl.when(block != 0)
        def _():
            copy.wait_send()

    out_tf.wait()
    out_branch.wait()
    out_panel.wait()


def scratch_shapes():
    v = pltpu.VMEM
    shapes = [
        v((LEN, FB), BF),
        v((LEN, FB), BF),
        v((LEN, 128), F32),
        v((FB, 256), BF),
        v((FB, 2 * QW), BF),
        v((2 * QW, FB), BF),
        v((32, 128), F32),
        v((32, 128), F32),
    ]
    shapes += [v((512, w), BF) for w in WIDTHS]
    shapes += [v((512, w), BF) for w in WIDTHS]
    shapes += [v((512, w), F32) for w in WIDTHS]
    for _ in range(6):
        shapes += [v((128, w), BF) for w in WIDTHS]
    shapes += [v((128, w), F32) for w in WIDTHS]
    shapes += [v((128, w), BF) for w in WIDTHS]
    shapes += [v((3, 32, w), BF) for w in WIDTHS]
    shapes += [v((LEN, 256), BF), v((32, 128), F32), v((2, 256, HD), BF), v((32, LEN), F32)]
    shapes += [v((LEN, QW), BF)] * 2
    shapes += [v((LEN, FB), F32), v((LEN, FB), BF), v((8, 128, FB), BF), v((LEN, FB), BF), v((4, LEN, FB), BF)]
    dma = pltpu.SemaphoreType.DMA
    shapes += [dma((160,)), dma((160,)), dma((16,)), dma((8,)), dma((8,))]
    return shapes


def product_kernel(panel, gathered, branch, gram, cross):
    for right, out in ((gathered, gram), (branch, cross)):
        out[...] = lax.dot_general(
            panel[0], right[...], (((0,), (0,)), ((), ())), preferred_element_type=F32
        ) * (1.0 / LEN)


def products(panel, gathered, branch):
    whole = pl.BlockSpec((LEN, FB), lambda i: (0, 0))
    return pl.pallas_call(
        product_kernel,
        grid=(4,),
        out_shape=(jax.ShapeDtypeStruct((4 * FB, FB), F32),) * 2,
        in_specs=[pl.BlockSpec((1, LEN, FB), lambda i: (i, 0, 0)), whole, whole],
        out_specs=(pl.BlockSpec((FB, FB), lambda i: (i, 0)),) * 2,
        compiler_params=pltpu.CompilerParams(vmem_limit_bytes=60 * 2**20),
        name="products",
    )(panel, gathered, branch)


def per_device(tokens, norm_gain, query_weight, key_weight, value_weight, output_weight):
    cosine, sine = tables()
    anywhere = pl.BlockSpec(memory_space=pl.ANY)
    in_vmem = pl.BlockSpec(memory_space=pltpu.VMEM)
    gathered, panel, branch = pl.pallas_call(
        kernel,
        out_shape=(
            jax.ShapeDtypeStruct((LEN, FB), BF),
            jax.ShapeDtypeStruct((4, LEN, FB), BF),
            jax.ShapeDtypeStruct((LEN, FB), BF),
        ),
        in_specs=[anywhere, in_vmem] + [anywhere] * 6,
        out_specs=(anywhere,) * 3,
        scratch_shapes=scratch_shapes(),
        compiler_params=pltpu.CompilerParams(
            collective_id=0, has_side_effects=True, vmem_limit_bytes=58 * 2**20
        ),
        name="layer",
    )(
        tokens,
        norm_gain,
        key_weight,
        value_weight,
        query_weight,
        output_weight,
        jnp.asarray(cosine),
        jnp.asarray(sine),
    )
    return products(panel, gathered, branch)


def solution(mesh):
    return jax.shard_map(
        per_device,
        mesh=mesh,
        in_specs=(
            P("col", ("grp", "row")),
            P(("grp", "row")),
            P(("grp", "row"), "col"),
            P(("grp", "row"), "col"),
            P(("grp", "row"), "col"),
            P("col", ("grp", "row")),
        ),
        out_specs=(P("col", ("grp", "row")), P("col", ("grp", "row"))),
        check_vma=False,
    )
```

```python
import functools
import math

import jax
import jax.numpy as jnp
import numpy as np
from jax import lax
from jax.experimental import pallas as pl
from jax.experimental.pallas import tpu as pltpu
from jax.sharding import PartitionSpec as P

D = 16384
H = 128
HD = 128
LEN = 1024
MESH = pl.DeviceIdType.MESH
BF = jnp.bfloat16
F32 = jnp.float32
FB = 512
KVW = 384
QW = 1024
WIDTHS = (KVW, QW, QW)


def tables():
    half = HD // 2
    frequency = np.float32(500000.0) ** (-np.arange(half, dtype=np.float32) * np.float32(2.0 / HD))
    angles = np.arange(LEN, dtype=np.float32)[:, None] * frequency.astype(np.float32)[None, :]
    cosine = np.cos(angles.astype(np.float64)).astype(np.float32)
    sine = np.sin(angles.astype(np.float64)).astype(np.float32)
    return (
        np.concatenate([cosine, cosine], axis=1),
        np.concatenate([-sine, sine], axis=1),
    )


def strips(rows, step, body):
    def one(i, carry):
        body(pl.multiple_of(i * step, step))
        return carry

    lax.fori_loop(0, rows // step, one, 0)


class Move:
    def __init__(self, copy):
        self.copy, self.open = copy, True

    def start(self):
        self.copy.start()

    def wait_recv(self):
        self.open = False
        self.copy.wait_recv()

    def wait_send(self):
        self.copy.wait_send()


def kernel(tok, gain, wk_in, wv_in, wq_in, wo_in, cos_in, sin_in, tf_out, panel_out, branch_out, *scratch):
    names = iter(scratch)
    nxt = lambda: next(names)
    tf, xg, sq, wkv, wq, wo, cosv, sinv = [nxt() for _ in range(8)]
    sib_send = [nxt() for _ in range(3)]
    sib_recv = [nxt() for _ in range(3)]
    r1 = [nxt() for _ in range(3)]
    y_send_p = [nxt() for _ in range(3)]
    y_send_m = [nxt() for _ in range(3)]
    y_send_f = [nxt() for _ in range(3)]
    y_recv_p = [nxt() for _ in range(3)]
    y_recv_m = [nxt() for _ in range(3)]
    y_recv_f = [nxt() for _ in range(3)]
    s2 = [nxt() for _ in range(3)]
    z_send = [nxt() for _ in range(3)]
    z_recv = [nxt() for _ in range(3)]
    kv, rs_scale, qs, bias = [nxt() for _ in range(4)]
    att = [nxt() for _ in range(2)]
    acc, bsend, brecv, ball, panel = [nxt() for _ in range(5)]
    ssem, rsem, lsem, bssem, brsem = [nxt() for _ in range(5)]

    g = lax.axis_index("grp")
    row = lax.axis_index("row")
    c = lax.axis_index("col")
    y, zh = row // 4, row % 4
    x, zl = c // 2, c % 2

    def at_y(d):
        return {"row": ((y + d) % 4) * 4 + zh}

    def at_z(d):
        return {"row": y * 4 + (zh + d) % 4}

    def at_col(dx, dl):
        return {"col": ((x + dx) % 4) * 2 + (zl + dl) % 2}

    sibling = {"grp": 1 - g}
    col_offsets = [(0, 1), (1, 0), (3, 0), (1, 1), (3, 1), (2, 0), (2, 1)]

    local = []

    def load(src, dst):
        copy = pltpu.make_async_copy(src, dst, lsem.at[len(local)])
        copy.start()
        local.append(copy)
        return copy

    own_row = pl.multiple_of(g * 512 + y * 128 + zh * 32, 32)
    first_token = pl.multiple_of(((g * 4 + y + c) % 8) * 128 + zh * 32, 32)
    my_tokens = pl.ds(pl.multiple_of(c * 128, 128), 128)
    l_tok = load(tok, tf.at[my_tokens])
    l_k = load(wk_in, wkv.at[:, pl.ds(0, HD)])
    l_v = load(wv_in, wkv.at[:, pl.ds(HD, HD)])
    l_q = load(wq_in, wq)
    l_cos = load(cos_in.at[pl.ds(first_token, 32)], cosv)
    l_sin = load(sin_in.at[pl.ds(first_token, 32)], sinv)
    l_o = load(wo_in, wo)

    barrier = pltpu.get_barrier_semaphore()
    peers = [sibling] + [at_y(d) for d in (1, 2, 3)] + [at_z(d) for d in (1, 2, 3)]
    peers += [at_col(*o) for o in col_offsets]
    for peer in peers:
        pl.semaphore_signal(barrier, inc=1, device_id=peer, device_id_type=MESH)
    pl.semaphore_wait(barrier, len(peers))

    sends = []
    count = [0]

    def describe(src, dst, dev, index=None):
        if index is None:
            index = count[0]
            count[0] += 1
        return pltpu.make_async_remote_copy(
            src_ref=src,
            dst_ref=dst,
            send_sem=ssem.at[index],
            recv_sem=rsem.at[index],
            device_id=dev,
            device_id_type=MESH,
        )

    def send(src, dst, dev):
        copy = Move(describe(src, dst, dev))
        copy.start()
        sends.append(copy)
        return copy

    gather = [send(tok, tf.at[my_tokens], at_col(*o)) for o in col_offsets]
    positions = first_token + lax.broadcasted_iota(jnp.int32, (32, 128), 0)
    for v in range(8):
        keys_at = ((v + c) % 8) * 128 + lax.broadcasted_iota(jnp.int32, (32, 128), 1)
        bias[:, v * 128 : (v + 1) * 128] = jnp.where(keys_at <= positions, F32(0), F32(-1e30))

    panel_core = g == c // 4
    delta = (y - c % 4 + 4) % 4
    is_source = jnp.logical_and(panel_core, delta == 0)

    def quarter(d):
        return pl.ds(pl.multiple_of(((y + d) % 4) * 256, 256), 256)

    spread = [describe(tf.at[quarter(d)], panel.at[zh, quarter(d)], at_y(d)) for d in (1, 2, 3)]
    across = [describe(panel.at[zh, quarter(0)], panel.at[zh, quarter(0)], at_z(d)) for d in (1, 2, 3)]
    along = [describe(panel.at[:, quarter(0)], panel.at[:, quarter(0)], at_y(d)) for d in (1, 3)]
    relays = [
        describe(panel.at[p, quarter(d)], panel.at[p, quarter(d)], at_y(4 - d)) for p, d in ((pl.ds(0, 2), 3), (pl.ds(2, 2), 1))
    ]
    over = [describe(panel.at[:, quarter(d)], panel.at[:, quarter(d)], sibling) for d in (0, 3, 1, 2)]
    own_quarter = pltpu.make_async_copy(tf.at[quarter(0)], panel.at[zh, quarter(0)], lsem.at[len(local)])
    local.append(None)

    def panel_spread():
        out_tf.start()

        @pl.when(is_source)
        def _():
            for copy in spread:
                copy.start()
            own_quarter.start()

    def panel_across():
        @pl.when(is_source)
        def _():
            own_quarter.wait()

        for d in (1, 2, 3):
            @pl.when(jnp.logical_and(panel_core, delta == d))
            def _():
                spread[d - 1].wait_recv()

        @pl.when(panel_core)
        def _():
            for copy in across:
                copy.start()

    def panel_along():
        @pl.when(panel_core)
        def _():
            for copy in across:
                copy.wait_recv()
            for copy in along:
                copy.start()
            over[0].start()

    def panel_relay():
        @pl.when(panel_core)
        def _():
            for i in range(2):
                along[i].wait_recv()
                relays[i].start()
            over[1].start()
            over[2].start()

    def panel_last():
        @pl.when(panel_core)
        def _():
            for copy in relays:
                copy.wait_recv()
            over[3].start()

    def panel_end():
        @pl.when(is_source)
        def _():
            for copy in spread:
                copy.wait_send()

        @pl.when(panel_core)
        def _():
            for copy in across + along + relays + over:
                copy.wait_send()

        @pl.when(jnp.logical_not(panel_core))
        def _():
            for copy in over:
                copy.wait_recv()

    out_tf = pltpu.make_async_copy(tf, tf_out, lsem.at[len(local)])
    local.append(None)

    sib = [[], [], []]

    def arrive(i):
        dx, dl = ((0, 0), *col_offsets)[i]
        if i == 0:
            l_tok.wait()
        else:
            gather[i - 1].wait_recv()
        block = ((x + 4 - dx) % 4) * 2 + (zl + dl) % 2
        base = pl.multiple_of(block * 128, 128)
        slot = (block + 8 - c) % 8
        here = slot // 4 == g
        part = pl.ds(pl.multiple_of((slot % 4) * 128, 128), 128)

        def prepare(j):
            rows = pl.ds(pl.multiple_of(base + j, 32), 32)
            wide = tf[rows, :].astype(F32)
            xg[rows, :] = (wide * gain[...].astype(F32)[None, :]).astype(BF)
            square = wide * wide
            sq[rows, :] = square[:, 0:128] + square[:, 128:256] + square[:, 256:384] + square[:, 384:512]

        strips(128, 32, prepare)

        rows = pl.ds(base, 128)
        for k in range(3):
            def project(out):
                weights = wkv[...] if k == 0 else wq[:, (k - 1) * QW : k * QW]
                wide = weights.shape[1]
                out[part, 0:wide] = jnp.dot(xg[rows, :], weights, preferred_element_type=F32).astype(out.dtype)
                if k == 0:
                    out[part, 256:384] = sq[rows, :].astype(out.dtype)

            @pl.when(here)
            def _():
                project(r1[k])

            @pl.when(jnp.logical_not(here))
            def _():
                project(sib_send[k])

            copy = describe(sib_send[k].at[part], sib_recv[k].at[part], sibling)
            sib[k].append((here, copy))

            @pl.when(jnp.logical_not(here))
            def _():
                copy.start()

    def sib_end():
        for moves in sib:
            for here, copy in moves:
                @pl.when(jnp.logical_not(here))
                def _():
                    copy.wait_send()

    def y_rows(d):
        return pl.multiple_of(((y + d) % 4) * 128, 128)

    y_moves = [None] * 3

    def y_first(k):
        for here, copy in sib[k]:
            @pl.when(here)
            def _():
                copy.wait_recv()


        def pair(d, dst, start, rows):
            base = y_rows(d)

            def strip(i):
                r = pl.ds(pl.multiple_of(base + start + i, 16), 16)
                dst[pl.ds(pl.multiple_of(start + i, 16), 16), :] = (r1[k][r, :] + sib_recv[k][r, :].astype(F32)).astype(BF)

            strips(rows, 16, strip)

        top, low = pl.ds(0, 64), pl.ds(64, 64)
        pair(2, y_send_f[k], 0, 128)
        m1p = send(y_send_f[k].at[top], y_recv_f[k].at[top], at_y(1))
        m1m = send(y_send_f[k].at[low], y_recv_f[k].at[low], at_y(3))
        pair(1, y_send_p[k], 64, 64)
        m2p = send(y_send_p[k].at[low], y_recv_p[k].at[low], at_y(1))
        pair(3, y_send_m[k], 0, 64)
        m2m = send(y_send_m[k].at[top], y_recv_m[k].at[top], at_y(3))
        y_moves[k] = [m1p, m1m, m2p, m2m]

    def y_second(k):
        top, low = pl.ds(0, 64), pl.ds(64, 64)
        m1p, m1m = y_moves[k][:2]

        def relay(d, dst, start):
            base = y_rows(d)

            def strip(i):
                r = pl.ds(pl.multiple_of(base + start + i, 16), 16)
                f = pl.ds(pl.multiple_of(start + i, 16), 16)
                dst[f, :] = (r1[k][r, :] + sib_recv[k][r, :].astype(F32) + y_recv_f[k][f, :].astype(F32)).astype(BF)

            strips(64, 16, strip)

        m1p.wait_recv()
        relay(1, y_send_p[k], 0)
        m3p = send(y_send_p[k].at[top], y_recv_p[k].at[top], at_y(1))
        m1m.wait_recv()
        relay(3, y_send_m[k], 64)
        m3m = send(y_send_m[k].at[low], y_recv_m[k].at[low], at_y(3))
        y_moves[k] += [m3p, m3m]

    z_moves = [None] * 3

    def z_first(k):
        for copy in y_moves[k][2:]:
            copy.wait_recv()
        base = y_rows(0)

        def strip(i):
            r = pl.ds(pl.multiple_of(base + i, 16), 16)
            f = pl.ds(i, 16)
            total = r1[k][r, :] + sib_recv[k][r, :].astype(F32) + y_recv_p[k][f, :].astype(F32) + y_recv_m[k][f, :].astype(F32)
            s2[k][f, :] = total
            z_send[k][f, :] = total.astype(BF)

        strips(128, 16, strip)
        z_moves[k] = [
            send(z_send[k].at[pl.ds(pl.multiple_of(((zh + d) % 4) * 32, 32), 32)], z_recv[k].at[d - 1], at_z(d))
            for d in (2, 1, 3)
        ]

    def z_sum(k, columns):
        own = pl.ds(pl.multiple_of(zh * 32, 32), 32)
        return (
            s2[k][own, columns]
            + z_recv[k][0, :, columns].astype(F32)
            + z_recv[k][1, :, columns].astype(F32)
            + z_recv[k][2, :, columns].astype(F32)
        )

    def rotated(values):
        return values * cosv[...] + pltpu.roll(values, 64, 1) * sinv[...]

    kv_moves = {}
    block_rows = pl.multiple_of(g * 512 + y * 128, 128)
    half_rows = pl.multiple_of(g * 512, 512)

    def kv_finish():
        for copy in z_moves[0]:
            copy.wait_recv()
        squares = jnp.sum(z_sum(0, pl.ds(256, 128)), axis=1, keepdims=True)
        scale = lax.rsqrt(squares / D + 1e-05)
        rs_scale[...] = jnp.broadcast_to(scale, (32, 128))
        l_cos.wait()
        l_sin.wait()
        rows = pl.ds(own_row, 32)
        kv[rows, pl.ds(0, HD)] = rotated(z_sum(0, pl.ds(0, HD)) * scale).astype(BF)
        kv[rows, pl.ds(HD, HD)] = (z_sum(0, pl.ds(HD, HD)) * scale).astype(BF)
        kv_moves["z"] = [send(kv.at[rows], kv.at[rows], at_z(d)) for d in (2, 1, 3)]

    def kv_y():
        for copy in kv_moves["z"]:
            copy.wait_recv()
        rows = pl.ds(block_rows, 128)
        kv_moves["y"] = [send(kv.at[rows], kv.at[rows], at_y(d)) for d in (2, 1, 3)]

    def kv_sib():
        for copy in kv_moves["y"]:
            copy.wait_recv()
        rows = pl.ds(half_rows, 512)
        kv_moves["s"] = send(kv.at[rows], kv.at[rows], sibling)

    def kv_here():
        kv_moves["s"].wait_recv()

    att_moves = [{}, {}]

    def queries(k):
        for copy in z_moves[k]:
            copy.wait_recv()
        for h in range(8):
            value = z_sum(k, pl.ds(h * HD, HD)) * rs_scale[...]
            qs[k - 1, pl.ds(h * 32, 32), :] = rotated(value).astype(BF)

    def attention(k):
        n = 256
        for part in range(256 // n):
            scores = lax.dot_general(
                qs[k - 1, pl.ds(part * n, n), :], kv[:, pl.ds(0, HD)], (((1,), (1,)), ((), ())), preferred_element_type=F32
            ) * (1.0 / math.sqrt(HD))
            scores = (scores.reshape(n // 32, 32, LEN) + bias[...][None]).reshape(n, LEN)
            peak = jnp.max(scores, axis=1, keepdims=True)
            e = jnp.exp(scores - peak)
            probs = (e * (1.0 / jnp.sum(e, axis=1, keepdims=True))).astype(BF)
            value = jnp.dot(probs, kv[:, pl.ds(HD, HD)], preferred_element_type=F32).astype(BF)
            for h in range(n // 32):
                att[k - 1][pl.ds(own_row, 32), pl.ds((part * (n // 32) + h) * HD, HD)] = value[h * 32 : (h + 1) * 32, :]
        rows = pl.ds(own_row, 32)
        att_moves[k - 1]["z"] = [send(att[k - 1].at[rows], att[k - 1].at[rows], at_z(d)) for d in (2, 1, 3)]

    def rows_of(dg, dy, start=0, size=128):
        gg = (g + dg) % 2
        return pl.ds(pl.multiple_of(gg * 512 + ((y + dy) % 4) * 128 + start, 64), size)

    def att_y(a):
        m = att_moves[a]
        for copy in m["z"]:
            copy.wait_recv()
        rows = rows_of(0, 0)
        m["p"] = send(att[a].at[rows], att[a].at[rows], at_y(1))
        m["m"] = send(att[a].at[rows], att[a].at[rows], at_y(3))
        m["s0"] = send(att[a].at[rows], att[a].at[rows], sibling)

    def att_relay(a):
        m = att_moves[a]
        m["p"].wait_recv()
        rows = rows_of(0, 3, 0, 64)
        m["rp"] = send(att[a].at[rows], att[a].at[rows], at_y(1))
        m["m"].wait_recv()
        rows = rows_of(0, 1, 64, 64)
        m["rm"] = send(att[a].at[rows], att[a].at[rows], at_y(3))
        for name, d in (("s3", 3), ("s1", 1)):
            rows = rows_of(0, d)
            m[name] = send(att[a].at[rows], att[a].at[rows], sibling)

    def att_last(a):
        m = att_moves[a]
        m["rp"].wait_recv()
        m["rm"].wait_recv()
        rows = rows_of(0, 2)
        m["s2"] = send(att[a].at[rows], att[a].at[rows], sibling)

    def out_block(a, dg, dy):
        if dg == 1:
            att_moves[a][f"s{dy}"].wait_recv()
        rows = rows_of(dg, dy)
        value = jnp.dot(att[a][rows, :], wo[pl.ds(a * QW, QW), :], preferred_element_type=F32)
        if a == 0:
            acc[rows, :] = value
            return
        total = acc[rows, :] + value
        acc[rows, :] = total
        bsend[rows, :] = total.astype(BF)
        block = ((g + dg) % 2) * 4 + (y + dy) % 4
        index = len(branch_moves)
        copy = pltpu.make_async_remote_copy(
            src_ref=bsend.at[rows],
            dst_ref=brecv.at[c],
            send_sem=bssem.at[index],
            recv_sem=brsem.at[c],
            device_id={"col": (block + c) % 8},
            device_id_type=MESH,
        )
        branch_moves.append((block, copy))

        @pl.when(block != 0)
        def _():
            copy.start()

    branch_moves = []

    def branch_sum():
        for s in range(1, 8):
            src = (c + s) % 8
            pltpu.make_async_remote_copy(
                src_ref=bsend.at[pl.ds(0, 128)],
                dst_ref=brecv.at[src],
                send_sem=bssem.at[0],
                recv_sem=brsem.at[src],
                device_id={"col": src},
                device_id_type=MESH,
            ).wait_recv()

        def reduce_strip(i):
            r = pl.ds(pl.multiple_of(c * 128 + i, 16), 16)
            total = acc[pl.ds(i, 16), :]
            for s in range(1, 8):
                total = total + brecv[(c + s) % 8, pl.ds(i, 16), :].astype(F32)
            ball[r, :] = total.astype(BF)

        strips(128, 16, reduce_strip)
        last = [send(ball.at[my_tokens], ball.at[my_tokens], at_col(*o)) for o in reversed(col_offsets)]
        branch_last.extend(last)

    def branch_end():
        for copy in branch_last:
            copy.wait_recv()
        out_branch.start()

    branch_last = []
    out_branch = pltpu.make_async_copy(ball, branch_out, lsem.at[len(local)])
    local.append(None)
    out_panel = pltpu.make_async_copy(panel, panel_out, lsem.at[len(local)])
    local.append(None)

    def loaded(*copies):
        for copy in copies:
            copy.wait()

    plan = [
        (loaded, l_k, l_v, l_q),
        *[(arrive, i) for i in range(8)],
        (y_first, 0),
        (y_first, 1),
        (y_second, 0),
        (y_first, 2),
        (z_first, 0),
        (y_second, 1),
        (kv_finish,),
        (z_first, 1),
        (y_second, 2),
        (kv_y,),
        (queries, 1),
        (kv_sib,),
        (z_first, 2),
        (kv_here,),
        (panel_spread,),
        (attention, 1),
        (queries, 2),
        (att_y, 0),
        (attention, 2),
        (att_y, 1),
        (panel_across,),
        (loaded, l_o),
        (out_block, 0, 0, 0),
        (out_block, 1, 0, 0),
        (out_block, 0, 1, 0),
        (att_relay, 0),
        (out_block, 1, 1, 0),
        (out_block, 0, 0, 1),
        (out_block, 0, 0, 3),
        (att_relay, 1),
        (out_block, 1, 0, 1),
        (out_block, 1, 0, 3),
        (out_block, 0, 1, 1),
        (out_block, 0, 1, 3),
        (att_last, 0),
        (out_block, 1, 1, 1),
        (out_block, 1, 1, 3),
        (out_block, 0, 0, 2),
        (out_block, 0, 1, 2),
        (panel_along,),
        (att_last, 1),
        (out_block, 1, 0, 2),
        (out_block, 1, 1, 2),
        (branch_sum,),
        (panel_relay,),
        (panel_last,),
        (branch_end,),
        (panel_end,),
        (sib_end,),
    ]
    for stage, *values in plan:
        stage(*values)
    out_panel.start()
    for copy in sends:
        copy.wait_send()
    for block, copy in branch_moves:
        @pl.when(block != 0)
        def _():
            copy.wait_send()

    out_tf.wait()
    out_branch.wait()
    out_panel.wait()


def scratch_shapes():
    v = pltpu.VMEM
    shapes = [
        v((LEN, FB), BF),
        v((LEN, FB), BF),
        v((LEN, 128), F32),
        v((FB, 256), BF),
        v((FB, 2 * QW), BF),
        v((2 * QW, FB), BF),
        v((32, 128), F32),
        v((32, 128), F32),
    ]
    shapes += [v((512, w), BF) for w in WIDTHS]
    shapes += [v((512, w), BF) for w in WIDTHS]
    shapes += [v((512, w), F32) for w in WIDTHS]
    for _ in range(6):
        shapes += [v((128, w), BF) for w in WIDTHS]
    shapes += [v((128, w), F32) for w in WIDTHS]
    shapes += [v((128, w), BF) for w in WIDTHS]
    shapes += [v((3, 32, w), BF) for w in WIDTHS]
    shapes += [v((LEN, 256), BF), v((32, 128), F32), v((2, 256, HD), BF), v((32, LEN), F32)]
    shapes += [v((LEN, QW), BF)] * 2
    shapes += [v((LEN, FB), F32), v((LEN, FB), BF), v((8, 128, FB), BF), v((LEN, FB), BF), v((4, LEN, FB), BF)]
    dma = pltpu.SemaphoreType.DMA
    shapes += [dma((160,)), dma((160,)), dma((16,)), dma((8,)), dma((8,))]
    return shapes


def product_kernel(panel, gathered, branch, gram, cross):
    for right, out in ((gathered, gram), (branch, cross)):
        out[...] = lax.dot_general(
            panel[0], right[...], (((0,), (0,)), ((), ())), preferred_element_type=F32
        ) * (1.0 / LEN)


def products(panel, gathered, branch):
    whole = pl.BlockSpec((LEN, FB), lambda i: (0, 0))
    return pl.pallas_call(
        product_kernel,
        grid=(4,),
        out_shape=(jax.ShapeDtypeStruct((4 * FB, FB), F32),) * 2,
        in_specs=[pl.BlockSpec((1, LEN, FB), lambda i: (i, 0, 0)), whole, whole],
        out_specs=(pl.BlockSpec((FB, FB), lambda i: (i, 0)),) * 2,
        compiler_params=pltpu.CompilerParams(vmem_limit_bytes=60 * 2**20),
        name="products",
    )(panel, gathered, branch)


def per_device(tokens, norm_gain, query_weight, key_weight, value_weight, output_weight):
    cosine, sine = tables()
    anywhere = pl.BlockSpec(memory_space=pl.ANY)
    in_vmem = pl.BlockSpec(memory_space=pltpu.VMEM)
    gathered, panel, branch = pl.pallas_call(
        kernel,
        out_shape=(
            jax.ShapeDtypeStruct((LEN, FB), BF),
            jax.ShapeDtypeStruct((4, LEN, FB), BF),
            jax.ShapeDtypeStruct((LEN, FB), BF),
        ),
        in_specs=[anywhere, in_vmem] + [anywhere] * 6,
        out_specs=(anywhere,) * 3,
        scratch_shapes=scratch_shapes(),
        compiler_params=pltpu.CompilerParams(
            collective_id=0, has_side_effects=True, vmem_limit_bytes=58 * 2**20
        ),
        name="layer",
    )(
        tokens,
        norm_gain,
        key_weight,
        value_weight,
        query_weight,
        output_weight,
        jnp.asarray(cosine),
        jnp.asarray(sine),
    )
    return products(panel, gathered, branch)


def solution(mesh):
    return jax.shard_map(
        per_device,
        mesh=mesh,
        in_specs=(
            P("col", ("grp", "row")),
            P(("grp", "row")),
            P(("grp", "row"), "col"),
            P(("grp", "row"), "col"),
            P(("grp", "row"), "col"),
            P("col", ("grp", "row")),
        ),
        out_specs=(P("col", ("grp", "row")), P("col", ("grp", "row"))),
        check_vma=False,
    )
```

```python
import functools
import math

import jax
import jax.numpy as jnp
import numpy as np
from jax import lax
from jax.experimental import pallas as pl
from jax.experimental.pallas import tpu as pltpu
from jax.sharding import PartitionSpec as P

D = 16384
H = 128
HD = 128
LEN = 1024
MESH = pl.DeviceIdType.MESH
BF = jnp.bfloat16
F32 = jnp.float32
FB = 512
KVW = 384
QW = 1024
WIDTHS = (KVW, QW, QW)


def tables():
    half = HD // 2
    frequency = np.float32(500000.0) ** (-np.arange(half, dtype=np.float32) * np.float32(2.0 / HD))
    angles = np.arange(LEN, dtype=np.float32)[:, None] * frequency.astype(np.float32)[None, :]
    cosine = np.cos(angles.astype(np.float64)).astype(np.float32)
    sine = np.sin(angles.astype(np.float64)).astype(np.float32)
    return (
        np.concatenate([cosine, cosine], axis=1),
        np.concatenate([-sine, sine], axis=1),
    )


def strips(rows, step, body):
    def one(i, carry):
        body(pl.multiple_of(i * step, step))
        return carry

    lax.fori_loop(0, rows // step, one, 0)


class Move:
    def __init__(self, copy):
        self.copy, self.open = copy, True

    def start(self):
        self.copy.start()

    def wait_recv(self):
        self.open = False
        self.copy.wait_recv()

    def wait_send(self):
        self.copy.wait_send()


def kernel(tok, gain, wk_in, wv_in, wq_in, wo_in, cos_in, sin_in, tf_out, panel_out, branch_out, *scratch):
    names = iter(scratch)
    nxt = lambda: next(names)
    tf, xg, sq, wkv, wq, wo, cosv, sinv = [nxt() for _ in range(8)]
    sib_send = [nxt() for _ in range(3)]
    sib_recv = [nxt() for _ in range(3)]
    r1 = [nxt() for _ in range(3)]
    y_send_p = [nxt() for _ in range(3)]
    y_send_m = [nxt() for _ in range(3)]
    y_send_f = [nxt() for _ in range(3)]
    y_recv_p = [nxt() for _ in range(3)]
    y_recv_m = [nxt() for _ in range(3)]
    y_recv_f = [nxt() for _ in range(3)]
    s2 = [nxt() for _ in range(3)]
    z_send = [nxt() for _ in range(3)]
    z_recv = [nxt() for _ in range(3)]
    kv, rs_scale, qs, bias = [nxt() for _ in range(4)]
    att = [nxt() for _ in range(2)]
    acc, bsend, brecv, ball, panel = [nxt() for _ in range(5)]
    ssem, rsem, lsem, bssem, brsem = [nxt() for _ in range(5)]

    g = lax.axis_index("grp")
    row = lax.axis_index("row")
    c = lax.axis_index("col")
    y, zh = row // 4, row % 4
    x, zl = c // 2, c % 2

    def at_y(d):
        return {"row": ((y + d) % 4) * 4 + zh}

    def at_z(d):
        return {"row": y * 4 + (zh + d) % 4}

    def at_col(dx, dl):
        return {"col": ((x + dx) % 4) * 2 + (zl + dl) % 2}

    sibling = {"grp": 1 - g}
    col_offsets = [(0, 1), (1, 0), (3, 0), (1, 1), (3, 1), (2, 0), (2, 1)]

    local = []

    def load(src, dst):
        copy = pltpu.make_async_copy(src, dst, lsem.at[len(local)])
        copy.start()
        local.append(copy)
        return copy

    own_row = pl.multiple_of(g * 512 + y * 128 + zh * 32, 32)
    first_token = pl.multiple_of(((g * 4 + y + c) % 8) * 128 + zh * 32, 32)
    my_tokens = pl.ds(pl.multiple_of(c * 128, 128), 128)
    l_tok = load(tok, tf.at[my_tokens])
    l_k = load(wk_in, wkv.at[:, pl.ds(0, HD)])
    l_v = load(wv_in, wkv.at[:, pl.ds(HD, HD)])
    l_q = load(wq_in, wq)
    l_cos = load(cos_in.at[pl.ds(first_token, 32)], cosv)
    l_sin = load(sin_in.at[pl.ds(first_token, 32)], sinv)
    l_o = load(wo_in, wo)

    barrier = pltpu.get_barrier_semaphore()
    peers = [sibling] + [at_y(d) for d in (1, 2, 3)] + [at_z(d) for d in (1, 2, 3)]
    peers += [at_col(*o) for o in col_offsets]
    for peer in peers:
        pl.semaphore_signal(barrier, inc=1, device_id=peer, device_id_type=MESH)
    pl.semaphore_wait(barrier, len(peers))

    sends = []
    count = [0]

    def describe(src, dst, dev, index=None):
        if index is None:
            index = count[0]
            count[0] += 1
        return pltpu.make_async_remote_copy(
            src_ref=src,
            dst_ref=dst,
            send_sem=ssem.at[index],
            recv_sem=rsem.at[index],
            device_id=dev,
            device_id_type=MESH,
        )

    def send(src, dst, dev):
        copy = Move(describe(src, dst, dev))
        copy.start()
        sends.append(copy)
        return copy

    gather = [send(tok, tf.at[my_tokens], at_col(*o)) for o in col_offsets]
    positions = first_token + lax.broadcasted_iota(jnp.int32, (32, 128), 0)
    for v in range(8):
        keys_at = ((v + c) % 8) * 128 + lax.broadcasted_iota(jnp.int32, (32, 128), 1)
        bias[:, v * 128 : (v + 1) * 128] = jnp.where(keys_at <= positions, F32(0), F32(-1e30))

    panel_core = g == c // 4
    delta = (y - c % 4 + 4) % 4
    is_source = jnp.logical_and(panel_core, delta == 0)

    def quarter(d):
        return pl.ds(pl.multiple_of(((y + d) % 4) * 256, 256), 256)

    spread = [describe(tf.at[quarter(d)], panel.at[zh, quarter(d)], at_y(d)) for d in (1, 2, 3)]
    across = [describe(panel.at[zh, quarter(0)], panel.at[zh, quarter(0)], at_z(d)) for d in (1, 2, 3)]
    along = [describe(panel.at[:, quarter(0)], panel.at[:, quarter(0)], at_y(d)) for d in (1, 3)]
    relays = [
        describe(panel.at[p, quarter(d)], panel.at[p, quarter(d)], at_y(4 - d)) for p, d in ((pl.ds(0, 2), 3), (pl.ds(2, 2), 1))
    ]
    over = [describe(panel.at[:, quarter(d)], panel.at[:, quarter(d)], sibling) for d in (0, 3, 1, 2)]
    own_quarter = pltpu.make_async_copy(tf.at[quarter(0)], panel.at[zh, quarter(0)], lsem.at[len(local)])
    local.append(None)

    def panel_spread():
        out_tf.start()

        @pl.when(is_source)
        def _():
            for copy in spread:
                copy.start()
            own_quarter.start()

    def panel_across():
        @pl.when(is_source)
        def _():
            own_quarter.wait()

        for d in (1, 2, 3):
            @pl.when(jnp.logical_and(panel_core, delta == d))
            def _():
                spread[d - 1].wait_recv()

        @pl.when(panel_core)
        def _():
            for copy in across:
                copy.start()

    def panel_along():
        @pl.when(panel_core)
        def _():
            for copy in across:
                copy.wait_recv()
            for copy in along:
                copy.start()
            over[0].start()

    def panel_relay():
        @pl.when(panel_core)
        def _():
            for i in range(2):
                along[i].wait_recv()
                relays[i].start()
            over[1].start()
            over[2].start()

    def panel_last():
        @pl.when(panel_core)
        def _():
            for copy in relays:
                copy.wait_recv()
            over[3].start()

    out_parts = []
    for d in (0, 3, 1, 2):
        out_parts.append(
            pltpu.make_async_copy(panel.at[:, quarter(d)], panel_out.at[:, quarter(d)], lsem.at[len(local)])
        )
        local.append(None)

    def panel_write():
        @pl.when(jnp.logical_not(panel_core))
        def _():
            for copy in over[:3]:
                copy.wait_recv()

        for copy in out_parts[:3]:
            copy.start()

    def panel_end():
        @pl.when(is_source)
        def _():
            for copy in spread:
                copy.wait_send()

        @pl.when(panel_core)
        def _():
            for copy in across + along + relays + over:
                copy.wait_send()

        @pl.when(jnp.logical_not(panel_core))
        def _():
            over[3].wait_recv()

    out_tf = pltpu.make_async_copy(tf, tf_out, lsem.at[len(local)])
    local.append(None)

    sib = [[], [], []]

    def arrive(i):
        dx, dl = ((0, 0), *col_offsets)[i]
        if i == 0:
            l_tok.wait()
        else:
            gather[i - 1].wait_recv()
        block = ((x + 4 - dx) % 4) * 2 + (zl + dl) % 2
        base = pl.multiple_of(block * 128, 128)
        slot = (block + 8 - c) % 8
        here = slot // 4 == g
        part = pl.ds(pl.multiple_of((slot % 4) * 128, 128), 128)

        def prepare(j):
            rows = pl.ds(pl.multiple_of(base + j, 32), 32)
            wide = tf[rows, :].astype(F32)
            xg[rows, :] = (wide * gain[...].astype(F32)[None, :]).astype(BF)
            square = wide * wide
            sq[rows, :] = square[:, 0:128] + square[:, 128:256] + square[:, 256:384] + square[:, 384:512]

        strips(128, 32, prepare)

        rows = pl.ds(base, 128)
        for k in range(3):
            def project(out):
                weights = wkv[...] if k == 0 else wq[:, (k - 1) * QW : k * QW]
                wide = weights.shape[1]
                out[part, 0:wide] = jnp.dot(xg[rows, :], weights, preferred_element_type=F32).astype(out.dtype)
                if k == 0:
                    out[part, 256:384] = sq[rows, :].astype(out.dtype)

            @pl.when(here)
            def _():
                project(r1[k])

            @pl.when(jnp.logical_not(here))
            def _():
                project(sib_send[k])

            copy = describe(sib_send[k].at[part], sib_recv[k].at[part], sibling)
            sib[k].append((here, copy))

            @pl.when(jnp.logical_not(here))
            def _():
                copy.start()

    def sib_end():
        for moves in sib:
            for here, copy in moves:
                @pl.when(jnp.logical_not(here))
                def _():
                    copy.wait_send()

    def y_rows(d):
        return pl.multiple_of(((y + d) % 4) * 128, 128)

    y_moves = [None] * 3

    def y_first(k):
        for here, copy in sib[k]:
            @pl.when(here)
            def _():
                copy.wait_recv()


        def pair(d, dst, start, rows):
            base = y_rows(d)

            def strip(i):
                r = pl.ds(pl.multiple_of(base + start + i, 16), 16)
                dst[pl.ds(pl.multiple_of(start + i, 16), 16), :] = (r1[k][r, :] + sib_recv[k][r, :].astype(F32)).astype(BF)

            strips(rows, 16, strip)

        top, low = pl.ds(0, 64), pl.ds(64, 64)
        pair(2, y_send_f[k], 0, 128)
        m1p = send(y_send_f[k].at[top], y_recv_f[k].at[top], at_y(1))
        m1m = send(y_send_f[k].at[low], y_recv_f[k].at[low], at_y(3))
        pair(1, y_send_p[k], 64, 64)
        m2p = send(y_send_p[k].at[low], y_recv_p[k].at[low], at_y(1))
        pair(3, y_send_m[k], 0, 64)
        m2m = send(y_send_m[k].at[top], y_recv_m[k].at[top], at_y(3))
        y_moves[k] = [m1p, m1m, m2p, m2m]

    def y_second(k):
        top, low = pl.ds(0, 64), pl.ds(64, 64)
        m1p, m1m = y_moves[k][:2]

        def relay(d, dst, start):
            base = y_rows(d)

            def strip(i):
                r = pl.ds(pl.multiple_of(base + start + i, 16), 16)
                f = pl.ds(pl.multiple_of(start + i, 16), 16)
                dst[f, :] = (r1[k][r, :] + sib_recv[k][r, :].astype(F32) + y_recv_f[k][f, :].astype(F32)).astype(BF)

            strips(64, 16, strip)

        m1p.wait_recv()
        relay(1, y_send_p[k], 0)
        m3p = send(y_send_p[k].at[top], y_recv_p[k].at[top], at_y(1))
        m1m.wait_recv()
        relay(3, y_send_m[k], 64)
        m3m = send(y_send_m[k].at[low], y_recv_m[k].at[low], at_y(3))
        y_moves[k] += [m3p, m3m]

    z_moves = [None] * 3

    def z_first(k):
        for copy in y_moves[k][2:]:
            copy.wait_recv()
        base = y_rows(0)

        def strip(i):
            r = pl.ds(pl.multiple_of(base + i, 16), 16)
            f = pl.ds(i, 16)
            total = r1[k][r, :] + sib_recv[k][r, :].astype(F32) + y_recv_p[k][f, :].astype(F32) + y_recv_m[k][f, :].astype(F32)
            s2[k][f, :] = total
            z_send[k][f, :] = total.astype(BF)

        strips(128, 16, strip)
        z_moves[k] = [
            send(z_send[k].at[pl.ds(pl.multiple_of(((zh + d) % 4) * 32, 32), 32)], z_recv[k].at[d - 1], at_z(d))
            for d in (2, 1, 3)
        ]

    def z_sum(k, columns):
        own = pl.ds(pl.multiple_of(zh * 32, 32), 32)
        return (
            s2[k][own, columns]
            + z_recv[k][0, :, columns].astype(F32)
            + z_recv[k][1, :, columns].astype(F32)
            + z_recv[k][2, :, columns].astype(F32)
        )

    def rotated(values):
        return values * cosv[...] + pltpu.roll(values, 64, 1) * sinv[...]

    kv_moves = {}
    block_rows = pl.multiple_of(g * 512 + y * 128, 128)
    half_rows = pl.multiple_of(g * 512, 512)

    def kv_finish():
        for copy in z_moves[0]:
            copy.wait_recv()
        squares = jnp.sum(z_sum(0, pl.ds(256, 128)), axis=1, keepdims=True)
        scale = lax.rsqrt(squares / D + 1e-05)
        rs_scale[...] = jnp.broadcast_to(scale, (32, 128))
        l_cos.wait()
        l_sin.wait()
        rows = pl.ds(own_row, 32)
        kv[rows, pl.ds(0, HD)] = rotated(z_sum(0, pl.ds(0, HD)) * scale).astype(BF)
        kv[rows, pl.ds(HD, HD)] = (z_sum(0, pl.ds(HD, HD)) * scale).astype(BF)
        kv_moves["z"] = [send(kv.at[rows], kv.at[rows], at_z(d)) for d in (2, 1, 3)]

    def kv_y():
        for copy in kv_moves["z"]:
            copy.wait_recv()
        rows = pl.ds(block_rows, 128)
        kv_moves["y"] = [send(kv.at[rows], kv.at[rows], at_y(d)) for d in (2, 1, 3)]

    def kv_sib():
        for copy in kv_moves["y"]:
            copy.wait_recv()
        rows = pl.ds(half_rows, 512)
        kv_moves["s"] = send(kv.at[rows], kv.at[rows], sibling)

    def kv_here():
        kv_moves["s"].wait_recv()

    att_moves = [{}, {}]

    def queries(k):
        for copy in z_moves[k]:
            copy.wait_recv()
        for h in range(8):
            value = z_sum(k, pl.ds(h * HD, HD)) * rs_scale[...]
            qs[k - 1, pl.ds(h * 32, 32), :] = rotated(value).astype(BF)

    def attention(k):
        n = 256
        for part in range(256 // n):
            scores = lax.dot_general(
                qs[k - 1, pl.ds(part * n, n), :], kv[:, pl.ds(0, HD)], (((1,), (1,)), ((), ())), preferred_element_type=F32
            ) * (1.0 / math.sqrt(HD))
            scores = (scores.reshape(n // 32, 32, LEN) + bias[...][None]).reshape(n, LEN)
            peak = jnp.max(scores, axis=1, keepdims=True)
            e = jnp.exp(scores - peak)
            probs = (e * (1.0 / jnp.sum(e, axis=1, keepdims=True))).astype(BF)
            value = jnp.dot(probs, kv[:, pl.ds(HD, HD)], preferred_element_type=F32).astype(BF)
            for h in range(n // 32):
                att[k - 1][pl.ds(own_row, 32), pl.ds((part * (n // 32) + h) * HD, HD)] = value[h * 32 : (h + 1) * 32, :]
        rows = pl.ds(own_row, 32)
        att_moves[k - 1]["z"] = [send(att[k - 1].at[rows], att[k - 1].at[rows], at_z(d)) for d in (2, 1, 3)]

    def rows_of(dg, dy, start=0, size=128):
        gg = (g + dg) % 2
        return pl.ds(pl.multiple_of(gg * 512 + ((y + dy) % 4) * 128 + start, 64), size)

    def att_y(a):
        m = att_moves[a]
        for copy in m["z"]:
            copy.wait_recv()
        rows = rows_of(0, 0)
        m["p"] = send(att[a].at[rows], att[a].at[rows], at_y(1))
        m["m"] = send(att[a].at[rows], att[a].at[rows], at_y(3))
        m["s0"] = send(att[a].at[rows], att[a].at[rows], sibling)

    def att_relay(a):
        m = att_moves[a]
        m["p"].wait_recv()
        rows = rows_of(0, 3, 0, 64)
        m["rp"] = send(att[a].at[rows], att[a].at[rows], at_y(1))
        m["m"].wait_recv()
        rows = rows_of(0, 1, 64, 64)
        m["rm"] = send(att[a].at[rows], att[a].at[rows], at_y(3))
        for name, d in (("s3", 3), ("s1", 1)):
            rows = rows_of(0, d)
            m[name] = send(att[a].at[rows], att[a].at[rows], sibling)

    def att_last(a):
        m = att_moves[a]
        m["rp"].wait_recv()
        m["rm"].wait_recv()
        rows = rows_of(0, 2)
        m["s2"] = send(att[a].at[rows], att[a].at[rows], sibling)

    def out_block(a, dg, dy):
        if dg == 1:
            att_moves[a][f"s{dy}"].wait_recv()
        rows = rows_of(dg, dy)
        value = jnp.dot(att[a][rows, :], wo[pl.ds(a * QW, QW), :], preferred_element_type=F32)
        if a == 0:
            acc[rows, :] = value
            return
        total = acc[rows, :] + value
        acc[rows, :] = total
        bsend[rows, :] = total.astype(BF)
        block = ((g + dg) % 2) * 4 + (y + dy) % 4
        index = len(branch_moves)
        copy = pltpu.make_async_remote_copy(
            src_ref=bsend.at[rows],
            dst_ref=brecv.at[c],
            send_sem=bssem.at[index],
            recv_sem=brsem.at[c],
            device_id={"col": (block + c) % 8},
            device_id_type=MESH,
        )
        branch_moves.append((block, copy))

        @pl.when(block != 0)
        def _():
            copy.start()

    branch_moves = []

    def branch_sum():
        for s in range(1, 8):
            src = (c + s) % 8
            pltpu.make_async_remote_copy(
                src_ref=bsend.at[pl.ds(0, 128)],
                dst_ref=brecv.at[src],
                send_sem=bssem.at[0],
                recv_sem=brsem.at[src],
                device_id={"col": src},
                device_id_type=MESH,
            ).wait_recv()

        def reduce_strip(i):
            r = pl.ds(pl.multiple_of(c * 128 + i, 16), 16)
            total = acc[pl.ds(i, 16), :]
            for s in range(1, 8):
                total = total + brecv[(c + s) % 8, pl.ds(i, 16), :].astype(F32)
            ball[r, :] = total.astype(BF)

        strips(128, 16, reduce_strip)
        last = [send(ball.at[my_tokens], ball.at[my_tokens], at_col(*o)) for o in reversed(col_offsets)]
        branch_last.extend(last)

    def branch_end():
        for copy in branch_last:
            copy.wait_recv()
        out_branch.start()

    branch_last = []
    out_branch = pltpu.make_async_copy(ball, branch_out, lsem.at[len(local)])
    local.append(None)
    def loaded(*copies):
        for copy in copies:
            copy.wait()

    plan = [
        (loaded, l_k, l_v, l_q),
        *[(arrive, i) for i in range(8)],
        (y_first, 0),
        (y_first, 1),
        (y_second, 0),
        (y_first, 2),
        (z_first, 0),
        (y_second, 1),
        (kv_finish,),
        (z_first, 1),
        (y_second, 2),
        (kv_y,),
        (queries, 1),
        (kv_sib,),
        (z_first, 2),
        (kv_here,),
        (panel_spread,),
        (attention, 1),
        (queries, 2),
        (att_y, 0),
        (attention, 2),
        (att_y, 1),
        (panel_across,),
        (loaded, l_o),
        (out_block, 0, 0, 0),
        (out_block, 1, 0, 0),
        (out_block, 0, 1, 0),
        (att_relay, 0),
        (out_block, 1, 1, 0),
        (out_block, 0, 0, 1),
        (out_block, 0, 0, 3),
        (att_relay, 1),
        (out_block, 1, 0, 1),
        (out_block, 1, 0, 3),
        (out_block, 0, 1, 1),
        (out_block, 0, 1, 3),
        (att_last, 0),
        (out_block, 1, 1, 1),
        (out_block, 1, 1, 3),
        (out_block, 0, 0, 2),
        (out_block, 0, 1, 2),
        (panel_along,),
        (att_last, 1),
        (out_block, 1, 0, 2),
        (out_block, 1, 1, 2),
        (branch_sum,),
        (panel_relay,),
        (panel_last,),
        (panel_write,),
        (branch_end,),
        (panel_end,),
        (sib_end,),
    ]
    for stage, *values in plan:
        stage(*values)
    out_parts[3].start()
    for copy in sends:
        copy.wait_send()
    for block, copy in branch_moves:
        @pl.when(block != 0)
        def _():
            copy.wait_send()

    out_tf.wait()
    out_branch.wait()
    for copy in out_parts:
        copy.wait()


def scratch_shapes():
    v = pltpu.VMEM
    shapes = [
        v((LEN, FB), BF),
        v((LEN, FB), BF),
        v((LEN, 128), F32),
        v((FB, 256), BF),
        v((FB, 2 * QW), BF),
        v((2 * QW, FB), BF),
        v((32, 128), F32),
        v((32, 128), F32),
    ]
    shapes += [v((512, w), BF) for w in WIDTHS]
    shapes += [v((512, w), BF) for w in WIDTHS]
    shapes += [v((512, w), F32) for w in WIDTHS]
    for _ in range(6):
        shapes += [v((128, w), BF) for w in WIDTHS]
    shapes += [v((128, w), F32) for w in WIDTHS]
    shapes += [v((128, w), BF) for w in WIDTHS]
    shapes += [v((3, 32, w), BF) for w in WIDTHS]
    shapes += [v((LEN, 256), BF), v((32, 128), F32), v((2, 256, HD), BF), v((32, LEN), F32)]
    shapes += [v((LEN, QW), BF)] * 2
    shapes += [v((LEN, FB), F32), v((LEN, FB), BF), v((8, 128, FB), BF), v((LEN, FB), BF), v((4, LEN, FB), BF)]
    dma = pltpu.SemaphoreType.DMA
    shapes += [dma((160,)), dma((160,)), dma((16,)), dma((8,)), dma((8,))]
    return shapes


def product_kernel(panel, gathered, branch, gram, cross):
    for right, out in ((gathered, gram), (branch, cross)):
        out[...] = lax.dot_general(
            panel[0], right[...], (((0,), (0,)), ((), ())), preferred_element_type=F32
        ) * (1.0 / LEN)


def products(panel, gathered, branch):
    whole = pl.BlockSpec((LEN, FB), lambda i: (0, 0))
    return pl.pallas_call(
        product_kernel,
        grid=(4,),
        out_shape=(jax.ShapeDtypeStruct((4 * FB, FB), F32),) * 2,
        in_specs=[pl.BlockSpec((1, LEN, FB), lambda i: (i, 0, 0)), whole, whole],
        out_specs=(pl.BlockSpec((FB, FB), lambda i: (i, 0)),) * 2,
        compiler_params=pltpu.CompilerParams(vmem_limit_bytes=60 * 2**20),
        name="products",
    )(panel, gathered, branch)


def per_device(tokens, norm_gain, query_weight, key_weight, value_weight, output_weight):
    cosine, sine = tables()
    anywhere = pl.BlockSpec(memory_space=pl.ANY)
    in_vmem = pl.BlockSpec(memory_space=pltpu.VMEM)
    gathered, panel, branch = pl.pallas_call(
        kernel,
        out_shape=(
            jax.ShapeDtypeStruct((LEN, FB), BF),
            jax.ShapeDtypeStruct((4, LEN, FB), BF),
            jax.ShapeDtypeStruct((LEN, FB), BF),
        ),
        in_specs=[anywhere, in_vmem] + [anywhere] * 6,
        out_specs=(anywhere,) * 3,
        scratch_shapes=scratch_shapes(),
        compiler_params=pltpu.CompilerParams(
            collective_id=0, has_side_effects=True, vmem_limit_bytes=58 * 2**20
        ),
        name="layer",
    )(
        tokens,
        norm_gain,
        key_weight,
        value_weight,
        query_weight,
        output_weight,
        jnp.asarray(cosine),
        jnp.asarray(sine),
    )
    return products(panel, gathered, branch)


def solution(mesh):
    return jax.shard_map(
        per_device,
        mesh=mesh,
        in_specs=(
            P("col", ("grp", "row")),
            P(("grp", "row")),
            P(("grp", "row"), "col"),
            P(("grp", "row"), "col"),
            P(("grp", "row"), "col"),
            P("col", ("grp", "row")),
        ),
        out_specs=(P("col", ("grp", "row")), P("col", ("grp", "row"))),
        check_vma=False,
    )
```

```python
import functools
import math

import jax
import jax.numpy as jnp
import numpy as np
from jax import lax
from jax.experimental import pallas as pl
from jax.experimental.pallas import tpu as pltpu
from jax.sharding import PartitionSpec as P

D = 16384
H = 128
HD = 128
LEN = 1024
MESH = pl.DeviceIdType.MESH
BF = jnp.bfloat16
F32 = jnp.float32
FB = 512
KVW = 384
QW = 1024
WIDTHS = (KVW, QW, QW)


def tables():
    half = HD // 2
    frequency = np.float32(500000.0) ** (-np.arange(half, dtype=np.float32) * np.float32(2.0 / HD))
    angles = np.arange(LEN, dtype=np.float32)[:, None] * frequency.astype(np.float32)[None, :]
    cosine = np.cos(angles.astype(np.float64)).astype(np.float32)
    sine = np.sin(angles.astype(np.float64)).astype(np.float32)
    return (
        np.concatenate([cosine, cosine], axis=1),
        np.concatenate([-sine, sine], axis=1),
    )


def strips(rows, step, body):
    def one(i, carry):
        body(pl.multiple_of(i * step, step))
        return carry

    lax.fori_loop(0, rows // step, one, 0)


class Move:
    def __init__(self, copy):
        self.copy, self.open = copy, True

    def start(self):
        self.copy.start()

    def wait_recv(self):
        self.open = False
        self.copy.wait_recv()

    def wait_send(self):
        self.copy.wait_send()


def kernel(tok, gain, wk_in, wv_in, wq_in, wo_in, cos_in, sin_in, tf_out, panel_out, branch_out, *scratch):
    names = iter(scratch)
    nxt = lambda: next(names)
    tf, xg, sq, wkv, wq, wo, cosv, sinv = [nxt() for _ in range(8)]
    sib_send = [nxt() for _ in range(3)]
    sib_recv = [nxt() for _ in range(3)]
    r1 = [nxt() for _ in range(3)]
    y_send_p = [nxt() for _ in range(3)]
    y_send_m = [nxt() for _ in range(3)]
    y_send_f = [nxt() for _ in range(3)]
    y_recv_p = [nxt() for _ in range(3)]
    y_recv_m = [nxt() for _ in range(3)]
    y_recv_f = [nxt() for _ in range(3)]
    s2 = [nxt() for _ in range(3)]
    z_send = [nxt() for _ in range(3)]
    z_recv = [nxt() for _ in range(3)]
    kv, rs_scale, qs, bias = [nxt() for _ in range(4)]
    att = [nxt() for _ in range(2)]
    acc, bsend, brecv, ball, panel = [nxt() for _ in range(5)]
    ssem, rsem, lsem, bssem, brsem = [nxt() for _ in range(5)]

    g = lax.axis_index("grp")
    row = lax.axis_index("row")
    c = lax.axis_index("col")
    y, zh = row // 4, row % 4
    x, zl = c // 2, c % 2

    def at_y(d):
        return {"row": ((y + d) % 4) * 4 + zh}

    def at_z(d):
        return {"row": y * 4 + (zh + d) % 4}

    def at_col(dx, dl):
        return {"col": ((x + dx) % 4) * 2 + (zl + dl) % 2}

    sibling = {"grp": 1 - g}
    col_offsets = [(0, 1), (1, 0), (3, 0), (1, 1), (3, 1), (2, 0), (2, 1)]

    local = []

    def load(src, dst):
        copy = pltpu.make_async_copy(src, dst, lsem.at[len(local)])
        copy.start()
        local.append(copy)
        return copy

    own_row = pl.multiple_of(g * 512 + y * 128 + zh * 32, 32)
    first_token = pl.multiple_of(((g * 4 + y + c) % 8) * 128 + zh * 32, 32)
    my_tokens = pl.ds(pl.multiple_of(c * 128, 128), 128)
    l_tok = load(tok, tf.at[my_tokens])
    l_k = load(wk_in, wkv.at[:, pl.ds(0, HD)])
    l_v = load(wv_in, wkv.at[:, pl.ds(HD, HD)])
    l_q = load(wq_in, wq)
    l_cos = load(cos_in.at[pl.ds(first_token, 32)], cosv)
    l_sin = load(sin_in.at[pl.ds(first_token, 32)], sinv)
    l_o = load(wo_in, wo)

    barrier = pltpu.get_barrier_semaphore()
    peers = [sibling] + [at_y(d) for d in (1, 2, 3)] + [at_z(d) for d in (1, 2, 3)]
    peers += [at_col(*o) for o in col_offsets]
    for peer in peers:
        pl.semaphore_signal(barrier, inc=1, device_id=peer, device_id_type=MESH)
    pl.semaphore_wait(barrier, len(peers))

    sends = []
    count = [0]

    def describe(src, dst, dev, index=None):
        if index is None:
            index = count[0]
            count[0] += 1
        return pltpu.make_async_remote_copy(
            src_ref=src,
            dst_ref=dst,
            send_sem=ssem.at[index],
            recv_sem=rsem.at[index],
            device_id=dev,
            device_id_type=MESH,
        )

    def send(src, dst, dev):
        copy = Move(describe(src, dst, dev))
        copy.start()
        sends.append(copy)
        return copy

    gather = [send(tok, tf.at[my_tokens], at_col(*o)) for o in reversed(col_offsets)][::-1]
    positions = first_token + lax.broadcasted_iota(jnp.int32, (32, 128), 0)
    for v in range(8):
        keys_at = ((v + c) % 8) * 128 + lax.broadcasted_iota(jnp.int32, (32, 128), 1)
        bias[:, v * 128 : (v + 1) * 128] = jnp.where(keys_at <= positions, F32(0), F32(-1e30))

    panel_core = g == c // 4
    delta = (y - c % 4 + 4) % 4
    is_source = jnp.logical_and(panel_core, delta == 0)

    def quarter(d):
        return pl.ds(pl.multiple_of(((y + d) % 4) * 256, 256), 256)

    spread = [describe(tf.at[quarter(d)], panel.at[zh, quarter(d)], at_y(d)) for d in (1, 2, 3)]
    across = [describe(panel.at[zh, quarter(0)], panel.at[zh, quarter(0)], at_z(d)) for d in (1, 2, 3)]
    along = [describe(panel.at[:, quarter(0)], panel.at[:, quarter(0)], at_y(d)) for d in (1, 3)]
    relays = [
        describe(panel.at[p, quarter(d)], panel.at[p, quarter(d)], at_y(4 - d)) for p, d in ((pl.ds(0, 2), 3), (pl.ds(2, 2), 1))
    ]
    over = [describe(panel.at[:, quarter(d)], panel.at[:, quarter(d)], sibling) for d in (0, 3, 1, 2)]
    own_quarter = pltpu.make_async_copy(tf.at[quarter(0)], panel.at[zh, quarter(0)], lsem.at[len(local)])
    local.append(None)

    def panel_spread():
        out_tf.start()

        @pl.when(is_source)
        def _():
            for copy in spread:
                copy.start()
            own_quarter.start()

    def panel_across():
        @pl.when(is_source)
        def _():
            own_quarter.wait()

        for d in (1, 2, 3):
            @pl.when(jnp.logical_and(panel_core, delta == d))
            def _():
                spread[d - 1].wait_recv()

        @pl.when(panel_core)
        def _():
            for copy in across:
                copy.start()

    def panel_along():
        @pl.when(panel_core)
        def _():
            for copy in across:
                copy.wait_recv()
            for copy in along:
                copy.start()
            over[0].start()

    def panel_relay():
        @pl.when(panel_core)
        def _():
            for i in range(2):
                along[i].wait_recv()
                relays[i].start()
            over[1].start()
            over[2].start()

    def panel_last():
        @pl.when(panel_core)
        def _():
            for copy in relays:
                copy.wait_recv()
            over[3].start()

    out_parts = []
    for d in (0, 3, 1, 2):
        out_parts.append(
            pltpu.make_async_copy(panel.at[:, quarter(d)], panel_out.at[:, quarter(d)], lsem.at[len(local)])
        )
        local.append(None)

    def panel_write():
        @pl.when(jnp.logical_not(panel_core))
        def _():
            for copy in over[:3]:
                copy.wait_recv()

        for copy in out_parts[:3]:
            copy.start()

    def panel_end():
        @pl.when(is_source)
        def _():
            for copy in spread:
                copy.wait_send()

        @pl.when(panel_core)
        def _():
            for copy in across + along + relays + over:
                copy.wait_send()

        @pl.when(jnp.logical_not(panel_core))
        def _():
            over[3].wait_recv()

    out_tf = pltpu.make_async_copy(tf, tf_out, lsem.at[len(local)])
    local.append(None)

    sib = [[], [], []]

    def arrive(i):
        dx, dl = ((0, 0), *col_offsets)[i]
        if i == 0:
            l_tok.wait()
        else:
            gather[i - 1].wait_recv()
        block = ((x + 4 - dx) % 4) * 2 + (zl + dl) % 2
        base = pl.multiple_of(block * 128, 128)
        slot = (block + 8 - c) % 8
        here = slot // 4 == g
        part = pl.ds(pl.multiple_of((slot % 4) * 128, 128), 128)

        def prepare(j):
            rows = pl.ds(pl.multiple_of(base + j, 32), 32)
            wide = tf[rows, :].astype(F32)
            xg[rows, :] = (wide * gain[...].astype(F32)[None, :]).astype(BF)
            square = wide * wide
            sq[rows, :] = square[:, 0:128] + square[:, 128:256] + square[:, 256:384] + square[:, 384:512]

        strips(128, 32, prepare)

        rows = pl.ds(base, 128)
        for k in range(3):
            def project(out):
                weights = wkv[...] if k == 0 else wq[:, (k - 1) * QW : k * QW]
                wide = weights.shape[1]
                out[part, 0:wide] = jnp.dot(xg[rows, :], weights, preferred_element_type=F32).astype(out.dtype)
                if k == 0:
                    out[part, 256:384] = sq[rows, :].astype(out.dtype)

            @pl.when(here)
            def _():
                project(r1[k])

            @pl.when(jnp.logical_not(here))
            def _():
                project(sib_send[k])

            copy = describe(sib_send[k].at[part], sib_recv[k].at[part], sibling)
            sib[k].append((here, copy))

            @pl.when(jnp.logical_not(here))
            def _():
                copy.start()

    def sib_end():
        for moves in sib:
            for here, copy in moves:
                @pl.when(jnp.logical_not(here))
                def _():
                    copy.wait_send()

    def y_rows(d):
        return pl.multiple_of(((y + d) % 4) * 128, 128)

    y_moves = [None] * 3

    def y_first(k):
        for here, copy in sib[k]:
            @pl.when(here)
            def _():
                copy.wait_recv()


        def pair(d, dst, start, rows):
            base = y_rows(d)

            def strip(i):
                r = pl.ds(pl.multiple_of(base + start + i, 16), 16)
                dst[pl.ds(pl.multiple_of(start + i, 16), 16), :] = (r1[k][r, :] + sib_recv[k][r, :].astype(F32)).astype(BF)

            strips(rows, 16, strip)

        top, low = pl.ds(0, 64), pl.ds(64, 64)
        pair(2, y_send_f[k], 0, 128)
        m1p = send(y_send_f[k].at[top], y_recv_f[k].at[top], at_y(1))
        m1m = send(y_send_f[k].at[low], y_recv_f[k].at[low], at_y(3))
        pair(1, y_send_p[k], 64, 64)
        m2p = send(y_send_p[k].at[low], y_recv_p[k].at[low], at_y(1))
        pair(3, y_send_m[k], 0, 64)
        m2m = send(y_send_m[k].at[top], y_recv_m[k].at[top], at_y(3))
        y_moves[k] = [m1p, m1m, m2p, m2m]

    def y_second(k):
        top, low = pl.ds(0, 64), pl.ds(64, 64)
        m1p, m1m = y_moves[k][:2]

        def relay(d, dst, start):
            base = y_rows(d)

            def strip(i):
                r = pl.ds(pl.multiple_of(base + start + i, 16), 16)
                f = pl.ds(pl.multiple_of(start + i, 16), 16)
                dst[f, :] = (r1[k][r, :] + sib_recv[k][r, :].astype(F32) + y_recv_f[k][f, :].astype(F32)).astype(BF)

            strips(64, 16, strip)

        m1p.wait_recv()
        relay(1, y_send_p[k], 0)
        m3p = send(y_send_p[k].at[top], y_recv_p[k].at[top], at_y(1))
        m1m.wait_recv()
        relay(3, y_send_m[k], 64)
        m3m = send(y_send_m[k].at[low], y_recv_m[k].at[low], at_y(3))
        y_moves[k] += [m3p, m3m]

    z_moves = [None] * 3

    def z_first(k):
        for copy in y_moves[k][2:]:
            copy.wait_recv()
        base = y_rows(0)

        def strip(i):
            r = pl.ds(pl.multiple_of(base + i, 16), 16)
            f = pl.ds(i, 16)
            total = r1[k][r, :] + sib_recv[k][r, :].astype(F32) + y_recv_p[k][f, :].astype(F32) + y_recv_m[k][f, :].astype(F32)
            s2[k][f, :] = total
            z_send[k][f, :] = total.astype(BF)

        strips(128, 16, strip)
        z_moves[k] = [
            send(z_send[k].at[pl.ds(pl.multiple_of(((zh + d) % 4) * 32, 32), 32)], z_recv[k].at[d - 1], at_z(d))
            for d in (2, 1, 3)
        ]

    def z_sum(k, columns):
        own = pl.ds(pl.multiple_of(zh * 32, 32), 32)
        return (
            s2[k][own, columns]
            + z_recv[k][0, :, columns].astype(F32)
            + z_recv[k][1, :, columns].astype(F32)
            + z_recv[k][2, :, columns].astype(F32)
        )

    def rotated(values):
        return values * cosv[...] + pltpu.roll(values, 64, 1) * sinv[...]

    kv_moves = {}
    block_rows = pl.multiple_of(g * 512 + y * 128, 128)
    half_rows = pl.multiple_of(g * 512, 512)

    def kv_finish():
        for copy in z_moves[0]:
            copy.wait_recv()
        squares = jnp.sum(z_sum(0, pl.ds(256, 128)), axis=1, keepdims=True)
        scale = lax.rsqrt(squares / D + 1e-05)
        rs_scale[...] = jnp.broadcast_to(scale, (32, 128))
        l_cos.wait()
        l_sin.wait()
        rows = pl.ds(own_row, 32)
        kv[rows, pl.ds(0, HD)] = rotated(z_sum(0, pl.ds(0, HD)) * scale).astype(BF)
        kv[rows, pl.ds(HD, HD)] = (z_sum(0, pl.ds(HD, HD)) * scale).astype(BF)
        kv_moves["z"] = [send(kv.at[rows], kv.at[rows], at_z(d)) for d in (2, 1, 3)]

    def kv_y():
        for copy in kv_moves["z"]:
            copy.wait_recv()
        rows = pl.ds(block_rows, 128)
        kv_moves["y"] = [send(kv.at[rows], kv.at[rows], at_y(d)) for d in (2, 1, 3)]

    def kv_sib():
        for copy in kv_moves["y"]:
            copy.wait_recv()
        rows = pl.ds(half_rows, 512)
        kv_moves["s"] = send(kv.at[rows], kv.at[rows], sibling)

    def kv_here():
        kv_moves["s"].wait_recv()

    att_moves = [{}, {}]

    def queries(k):
        for copy in z_moves[k]:
            copy.wait_recv()
        for h in range(8):
            value = z_sum(k, pl.ds(h * HD, HD)) * rs_scale[...]
            qs[k - 1, pl.ds(h * 32, 32), :] = rotated(value).astype(BF)

    def attention(k):
        n = 256
        for part in range(256 // n):
            scores = lax.dot_general(
                qs[k - 1, pl.ds(part * n, n), :], kv[:, pl.ds(0, HD)], (((1,), (1,)), ((), ())), preferred_element_type=F32
            ) * (1.0 / math.sqrt(HD))
            scores = (scores.reshape(n // 32, 32, LEN) + bias[...][None]).reshape(n, LEN)
            peak = jnp.max(scores, axis=1, keepdims=True)
            e = jnp.exp(scores - peak)
            probs = (e * (1.0 / jnp.sum(e, axis=1, keepdims=True))).astype(BF)
            value = jnp.dot(probs, kv[:, pl.ds(HD, HD)], preferred_element_type=F32).astype(BF)
            for h in range(n // 32):
                att[k - 1][pl.ds(own_row, 32), pl.ds((part * (n // 32) + h) * HD, HD)] = value[h * 32 : (h + 1) * 32, :]
        rows = pl.ds(own_row, 32)
        att_moves[k - 1]["z"] = [send(att[k - 1].at[rows], att[k - 1].at[rows], at_z(d)) for d in (2, 1, 3)]

    def rows_of(dg, dy, start=0, size=128):
        gg = (g + dg) % 2
        return pl.ds(pl.multiple_of(gg * 512 + ((y + dy) % 4) * 128 + start, 64), size)

    def att_y(a):
        m = att_moves[a]
        for copy in m["z"]:
            copy.wait_recv()
        rows = rows_of(0, 0)
        m["p"] = send(att[a].at[rows], att[a].at[rows], at_y(1))
        m["m"] = send(att[a].at[rows], att[a].at[rows], at_y(3))
        m["s0"] = send(att[a].at[rows], att[a].at[rows], sibling)

    def att_relay(a):
        m = att_moves[a]
        m["p"].wait_recv()
        rows = rows_of(0, 3, 0, 64)
        m["rp"] = send(att[a].at[rows], att[a].at[rows], at_y(1))
        m["m"].wait_recv()
        rows = rows_of(0, 1, 64, 64)
        m["rm"] = send(att[a].at[rows], att[a].at[rows], at_y(3))
        for name, d in (("s3", 3), ("s1", 1)):
            rows = rows_of(0, d)
            m[name] = send(att[a].at[rows], att[a].at[rows], sibling)

    def att_last(a):
        m = att_moves[a]
        m["rp"].wait_recv()
        m["rm"].wait_recv()
        rows = rows_of(0, 2)
        m["s2"] = send(att[a].at[rows], att[a].at[rows], sibling)

    def out_block(a, dg, dy):
        if dg == 1:
            att_moves[a][f"s{dy}"].wait_recv()
        rows = rows_of(dg, dy)
        value = jnp.dot(att[a][rows, :], wo[pl.ds(a * QW, QW), :], preferred_element_type=F32)
        if a == 0:
            acc[rows, :] = value
            return
        total = acc[rows, :] + value
        acc[rows, :] = total
        bsend[rows, :] = total.astype(BF)
        block = ((g + dg) % 2) * 4 + (y + dy) % 4
        index = len(branch_moves)
        copy = pltpu.make_async_remote_copy(
            src_ref=bsend.at[rows],
            dst_ref=brecv.at[c],
            send_sem=bssem.at[index],
            recv_sem=brsem.at[c],
            device_id={"col": (block + c) % 8},
            device_id_type=MESH,
        )
        branch_moves.append((block, copy))

        @pl.when(block != 0)
        def _():
            copy.start()

    branch_moves = []

    def branch_sum():
        for s in range(1, 8):
            src = (c + s) % 8
            pltpu.make_async_remote_copy(
                src_ref=bsend.at[pl.ds(0, 128)],
                dst_ref=brecv.at[src],
                send_sem=bssem.at[0],
                recv_sem=brsem.at[src],
                device_id={"col": src},
                device_id_type=MESH,
            ).wait_recv()

        def reduce_strip(i):
            r = pl.ds(pl.multiple_of(c * 128 + i, 16), 16)
            total = acc[pl.ds(i, 16), :]
            for s in range(1, 8):
                total = total + brecv[(c + s) % 8, pl.ds(i, 16), :].astype(F32)
            ball[r, :] = total.astype(BF)

        strips(128, 16, reduce_strip)
        last = [send(ball.at[my_tokens], ball.at[my_tokens], at_col(*o)) for o in reversed(col_offsets)]
        branch_last.extend(last)

    def branch_end():
        for copy in branch_last:
            copy.wait_recv()
        out_branch.start()

    branch_last = []
    out_branch = pltpu.make_async_copy(ball, branch_out, lsem.at[len(local)])
    local.append(None)
    def loaded(*copies):
        for copy in copies:
            copy.wait()

    plan = [
        (loaded, l_k, l_v, l_q),
        *[(arrive, i) for i in range(8)],
        (y_first, 0),
        (y_first, 1),
        (y_second, 0),
        (y_first, 2),
        (z_first, 0),
        (y_second, 1),
        (kv_finish,),
        (z_first, 1),
        (y_second, 2),
        (kv_y,),
        (queries, 1),
        (kv_sib,),
        (z_first, 2),
        (kv_here,),
        (panel_spread,),
        (attention, 1),
        (queries, 2),
        (att_y, 0),
        (attention, 2),
        (att_y, 1),
        (panel_across,),
        (loaded, l_o),
        (out_block, 0, 0, 0),
        (out_block, 1, 0, 0),
        (out_block, 0, 1, 0),
        (att_relay, 0),
        (out_block, 1, 1, 0),
        (out_block, 0, 0, 1),
        (out_block, 0, 0, 3),
        (att_relay, 1),
        (out_block, 1, 0, 1),
        (out_block, 1, 0, 3),
        (out_block, 0, 1, 1),
        (out_block, 0, 1, 3),
        (att_last, 0),
        (out_block, 1, 1, 1),
        (out_block, 1, 1, 3),
        (out_block, 0, 0, 2),
        (out_block, 0, 1, 2),
        (panel_along,),
        (att_last, 1),
        (out_block, 1, 0, 2),
        (out_block, 1, 1, 2),
        (branch_sum,),
        (panel_relay,),
        (panel_last,),
        (panel_write,),
        (branch_end,),
        (panel_end,),
        (sib_end,),
    ]
    for stage, *values in plan:
        stage(*values)
    out_parts[3].start()
    for copy in sends:
        copy.wait_send()
    for block, copy in branch_moves:
        @pl.when(block != 0)
        def _():
            copy.wait_send()

    out_tf.wait()
    out_branch.wait()
    for copy in out_parts:
        copy.wait()


def scratch_shapes():
    v = pltpu.VMEM
    shapes = [
        v((LEN, FB), BF),
        v((LEN, FB), BF),
        v((LEN, 128), F32),
        v((FB, 256), BF),
        v((FB, 2 * QW), BF),
        v((2 * QW, FB), BF),
        v((32, 128), F32),
        v((32, 128), F32),
    ]
    shapes += [v((512, w), BF) for w in WIDTHS]
    shapes += [v((512, w), BF) for w in WIDTHS]
    shapes += [v((512, w), F32) for w in WIDTHS]
    for _ in range(6):
        shapes += [v((128, w), BF) for w in WIDTHS]
    shapes += [v((128, w), F32) for w in WIDTHS]
    shapes += [v((128, w), BF) for w in WIDTHS]
    shapes += [v((3, 32, w), BF) for w in WIDTHS]
    shapes += [v((LEN, 256), BF), v((32, 128), F32), v((2, 256, HD), BF), v((32, LEN), F32)]
    shapes += [v((LEN, QW), BF)] * 2
    shapes += [v((LEN, FB), F32), v((LEN, FB), BF), v((8, 128, FB), BF), v((LEN, FB), BF), v((4, LEN, FB), BF)]
    dma = pltpu.SemaphoreType.DMA
    shapes += [dma((160,)), dma((160,)), dma((16,)), dma((8,)), dma((8,))]
    return shapes


def product_kernel(panel, gathered, branch, gram, cross):
    for right, out in ((gathered, gram), (branch, cross)):
        out[...] = lax.dot_general(
            panel[0], right[...], (((0,), (0,)), ((), ())), preferred_element_type=F32
        ) * (1.0 / LEN)


def products(panel, gathered, branch):
    whole = pl.BlockSpec((LEN, FB), lambda i: (0, 0))
    return pl.pallas_call(
        product_kernel,
        grid=(4,),
        out_shape=(jax.ShapeDtypeStruct((4 * FB, FB), F32),) * 2,
        in_specs=[pl.BlockSpec((1, LEN, FB), lambda i: (i, 0, 0)), whole, whole],
        out_specs=(pl.BlockSpec((FB, FB), lambda i: (i, 0)),) * 2,
        compiler_params=pltpu.CompilerParams(vmem_limit_bytes=60 * 2**20),
        name="products",
    )(panel, gathered, branch)


def per_device(tokens, norm_gain, query_weight, key_weight, value_weight, output_weight):
    cosine, sine = tables()
    anywhere = pl.BlockSpec(memory_space=pl.ANY)
    in_vmem = pl.BlockSpec(memory_space=pltpu.VMEM)
    gathered, panel, branch = pl.pallas_call(
        kernel,
        out_shape=(
            jax.ShapeDtypeStruct((LEN, FB), BF),
            jax.ShapeDtypeStruct((4, LEN, FB), BF),
            jax.ShapeDtypeStruct((LEN, FB), BF),
        ),
        in_specs=[anywhere, in_vmem] + [anywhere] * 6,
        out_specs=(anywhere,) * 3,
        scratch_shapes=scratch_shapes(),
        compiler_params=pltpu.CompilerParams(
            collective_id=0, has_side_effects=True, vmem_limit_bytes=58 * 2**20
        ),
        name="layer",
    )(
        tokens,
        norm_gain,
        key_weight,
        value_weight,
        query_weight,
        output_weight,
        jnp.asarray(cosine),
        jnp.asarray(sine),
    )
    return products(panel, gathered, branch)


def solution(mesh):
    return jax.shard_map(
        per_device,
        mesh=mesh,
        in_specs=(
            P("col", ("grp", "row")),
            P(("grp", "row")),
            P(("grp", "row"), "col"),
            P(("grp", "row"), "col"),
            P(("grp", "row"), "col"),
            P("col", ("grp", "row")),
        ),
        out_specs=(P("col", ("grp", "row")), P("col", ("grp", "row"))),
        check_vma=False,
    )
```
